128 devices in a mesh: rep: 32 (over x, z, core), head: 4 (over y).
Axes of the slice: x: 4, y: 4, z: 4, core: 2. Of those that a mesh axis runs over, the one named last changes fastest.
Arguments:
- query: bfloat16 [288, 64, 192], P('rep', 'head'), may hold values from -3 to 3
- latent_cache: bfloat16 [256, 512, 576], P('rep'), may hold values from -51 to 51
- moved_rows: bfloat16 [32, 3072, 576], P(None, ('rep', 'head')), may hold values from -51 to 51
- target_group: int32 [32], replicated, may hold values from 0 to 31, each once
- moved_length: int32 [32], replicated, may hold values from 2 to 3072, as said below
- key_absorb: bfloat16 [64, 128, 512], P('head'), may hold values from -0.5 to 0.5
- value_head_projection: bfloat16 [64, 512, 128], P('head'), may hold values from -0.25 to 0.25
- out_proj: bfloat16 [8192, 3584], P(None, ('rep', 'head')), may hold values from -1.5 to 1.5
- residual: bfloat16 [288, 3584], P(None, ('rep', 'head')), may hold values from -16 to 16
- norm_gain: bfloat16 [3584], P(('rep', 'head')), may hold values from 0.099609375 to 1.8984375
- centroid: bfloat16 [128, 3584], P(None, ('rep', 'head')), may hold values from -0.09375 to 0.09375
- expert_ids: int32 [288, 8], replicated, may hold values from 0 to 127, all different within a row; in each aligned block of 288 rows (0 to 287, 288 to 575, ...) at most 36 rows name the same one
- up_weight: bfloat16 [128, 3584, 1024], P(('rep', 'head')), may hold values from -0.09375 to 0.09375
- down_weight: bfloat16 [128, 1024, 3584], P(('rep', 'head')), may hold values from -0.1875 to 0.1875
Outputs:
- layer_out: bfloat16 [288, 3584], P(None, ('rep', 'head'))
The draws below stay inside these ranges and needn't reach their ends.
Inputs may be any that keep to these rules, and one draw needn't show every extreme that they name: `expert_ids`: each token names 8 different experts; over all tokens no expert is named by more than 36 rows, a bound that some block reaches. `target_group`: A permutation: every group receives exactly one migrated request. `moved_length`: some request has all 3072 rows valid.
All inputs are finite; a program needn't handle non-finite values.
Results may differ from the reference program's by a relative error of at most 0.0065.
Values may be sent and summed in bfloat16 or wider, within the bound.
A program may use at most 128 MiB of HBM per device.

```python
import math
import jax
import jax.numpy as jnp
import numpy as np
from jax import lax

H = 64
NOPE = 128
ROPE = 64
KV = 512
VD = 128
D = 3584
F = 1024
TOPK = 8
RES = 8
CTX = 512
BATCH = 9
TOKENS = 288
MIGLEN = 3072
EXPERTS = 128
CAP = 36
N_REP = 32


def draw_query(key, part):
    key = jax.random.fold_in(key, 11)
    base_values = 0.5 * jax.random.truncated_normal(key, -6.0, 6.0, (TOKENS, H, NOPE + ROPE))
    return base_values.astype(jnp.bfloat16)


def draw_latent_cache(key, part):
    key = jax.random.fold_in(key, 12)
    shape = (N_REP * RES, CTX, KV + ROPE)
    return jax.random.truncated_normal(key, -6.0, 6.0, shape).astype(jnp.bfloat16)


def draw_moved_rows(key, part):
    key = jax.random.fold_in(key, 13)
    shape = (N_REP, MIGLEN, KV + ROPE)
    return jax.random.truncated_normal(key, -6.0, 6.0, shape).astype(jnp.bfloat16)


def draw_moved_length(key, part):
    key = jax.random.fold_in(key, 14)
    first_key, second_key = jax.random.split(key)
    lengths = jax.random.randint(first_key, (N_REP,), 2, MIGLEN + 1)
    chosen_spot = jax.random.randint(second_key, (), 0, N_REP)
    return jnp.where(jnp.arange(N_REP) == chosen_spot, MIGLEN, lengths).astype(jnp.int32)


def draw_residual(key, part):
    key = jax.random.fold_in(key, 15)
    first_key = jax.random.fold_in(key, 0)
    base_values = jax.random.truncated_normal(first_key, -6.0, 6.0, (TOKENS, D))
    return base_values.astype(jnp.bfloat16)


def block_levels(key, shape, cuts, smallest, high):
    factor_of = 1.0
    for dim, blocks in cuts:
        steps = jax.random.uniform(jax.random.fold_in(jax.random.fold_in(key, 6), dim), (blocks,), jnp.float32, smallest / len(cuts), high / len(cuts))
        factor_of = factor_of * jnp.repeat(jnp.exp(steps), shape[dim] // blocks).reshape((-1,) + (1,) * (len(shape) - 1 - dim))
    return factor_of


def assign_block(key, own, number, rows, number_of, top, reach, skew):
    ranking = jax.random.permutation(key, number_of)
    heavy_load, usual = load_shares(number_of, rows * top, reach, skew, True), load_shares(number_of, rows * top, reach, skew, False)
    places = jnp.arange(number_of)

    def named(tallies, turn):
        used = int((tallies > 0).sum())
        fixed = max(1, used // 4)
        shifted = fixed + (places - fixed + turn * (used - fixed)) % max(1, number_of - fixed)
        return jnp.zeros((number_of,), jnp.int32).at[ranking[jnp.where(places < fixed, places, shifted)]].set(jnp.asarray(tallies, jnp.int32))

    tallies = jnp.where(number % 4 == 0, named(heavy_load, number // 4), named(usual, number - number // 4 - 1))
    mixed = jax.random.permutation(jax.random.fold_in(own, 3), number_of)
    donor, receiver = mixed[0:number_of // 2 * 2:2], mixed[1:number_of // 2 * 2:2]
    slack = jnp.minimum(tallies[donor] - 1, reach - tallies[receiver]) // 2
    slack = jnp.where((donor == ranking[0]) | (receiver == ranking[0]) | (tallies[receiver] == 0), 0, jnp.maximum(slack, 0))
    shifted = jax.random.randint(jax.random.fold_in(own, 4), (number_of // 2,), 0, 1 << 20) % (slack + 1)
    tallies = tallies.at[donor].add(-shifted).at[receiver].add(shifted)
    members = jnp.searchsorted(jnp.cumsum(tallies), jnp.arange(rows * top), side="right").astype(jnp.int32)
    grid = members.reshape(top, rows).T
    grid = grid[jax.random.permutation(jax.random.fold_in(own, 1), rows)]
    turn = jax.random.randint(jax.random.fold_in(own, 2), (rows, 1), 0, top)
    return jnp.take_along_axis(grid, (jnp.arange(top)[None, :] + turn) % top, axis=1)


def load_shares(count, total, most, skew, full):
    loads = [(1 << 20) // math.isqrt(grade ** skew) + 1 for grade in range(1, count + 1)]
    largest = most if full else min(most, max(-(-total // count), total * loads[0] // sum(loads)))
    least = 1 if total - largest >= count - 1 else 0
    counts, surplus = [largest] + [least] * (count - 1), total - largest - least * (count - 1)
    while surplus > 0:
        movable = [i for i in range(1, count) if counts[i] < largest] or [i for i in range(1, count) if counts[i] < most]
        pool, budget = sum([loads[i] for i in movable]), surplus
        for i in movable:
            addition = min(most - counts[i], max(1, budget * loads[i] // pool), surplus)
            counts[i] = counts[i] + addition
            surplus = surplus - addition
    return np.array(counts)


def bell_draw(key, extent, scale, bound, shards=(), kind=jnp.bfloat16):
    factor_of = block_levels(key, extent, shards, -0.22, 0.18) if shards else 1.0
    drawn = jax.random.normal(key, extent, jnp.float32) * scale * factor_of
    return jnp.minimum(jnp.maximum(drawn, -bound), bound).astype(kind)


def setup_inputs(seed: int = 0) -> dict:
    key_list = jax.random.split(jax.random.key(seed), 15)
    query = draw_query(jax.random.fold_in(key_list[14], 71), 0)
    latent_cache = draw_latent_cache(jax.random.fold_in(key_list[14], 71), 0)
    moved_rows = draw_moved_rows(jax.random.fold_in(key_list[14], 71), 0)
    target_group = jax.random.permutation(key_list[3], N_REP).astype(jnp.int32)
    moved_length = draw_moved_length(jax.random.fold_in(key_list[14], 71), 0)
    key_absorb = bell_draw(key_list[5], (H, NOPE, KV), NOPE ** -0.5, 0.5, ((0, 4),))
    value_head_projection = bell_draw(key_list[6], (H, KV, VD), KV ** -0.5, 0.25, ((0, 4),))
    out_proj = bell_draw(key_list[7], (H * VD, D), (max(1, H * VD // 512)) ** -0.5, 1.5, ((1, 128),))
    residual = draw_residual(jax.random.fold_in(key_list[14], 71), 0)
    norm_gain = jnp.clip(1.0 + 0.18 * jax.random.normal(key_list[9], (D,), jnp.float32), 0.099609375, 1.8984375).astype(jnp.bfloat16)
    centroid = bell_draw(key_list[10], (EXPERTS, D), D ** -0.5, 0.09375, ((1, 128),))
    expert_ids_keys = jax.random.split(jax.random.fold_in(key_list[11], 1), TOKENS // TOKENS)
    expert_ids_turns = jax.random.permutation(jax.random.fold_in(key_list[11], 3), TOKENS // TOKENS)
    expert_ids = jax.vmap(lambda own, number: assign_block(jax.random.fold_in(key_list[11], 2), own, number, TOKENS, EXPERTS, TOPK, CAP, 1))(expert_ids_keys, expert_ids_turns).reshape((TOKENS, TOPK))
    up_weight = bell_draw(key_list[12], (EXPERTS, D, F), D ** -0.5, 0.09375, ((0, 128),))
    down_weight = bell_draw(key_list[13], (EXPERTS, F, D), F ** -0.5, 0.1875, ((0, 128),))
    return dict(query=query, latent_cache=latent_cache, moved_rows=moved_rows, target_group=target_group, moved_length=moved_length, key_absorb=key_absorb, value_head_projection=value_head_projection, out_proj=out_proj, residual=residual, norm_gain=norm_gain, centroid=centroid, expert_ids=expert_ids, up_weight=up_weight, down_weight=down_weight)


def normalize(scores):
    highest = lax.optimization_barrier(jnp.max(scores, axis=-1, keepdims=True))
    routing_weights = jnp.exp(scores - highest)
    return (routing_weights / lax.optimization_barrier(jnp.sum(routing_weights, axis=-1, keepdims=True))).astype(jnp.bfloat16)

def expert_slots(expert_ids, experts):
    pair_expert = expert_ids.reshape(-1)
    matches = (pair_expert[:, None] == jnp.arange(experts, dtype=jnp.int32)[None, :]).astype(jnp.int32)
    running = jnp.cumsum(matches, axis=0) - 1
    pair_slot = lax.optimization_barrier(jnp.sum(running * matches, axis=1)).astype(jnp.int32)
    return (pair_expert, pair_slot)

def reference(query, latent_cache, moved_rows, target_group, moved_length, key_absorb, value_head_projection, out_proj, residual, norm_gain, centroid, expert_ids, up_weight, down_weight):
    scaling_factor = 1.0 / math.sqrt(NOPE + ROPE)
    source = jnp.zeros((N_REP,), jnp.int32).at[target_group].set(jnp.arange(N_REP, dtype=jnp.int32))
    group_query = query.reshape(N_REP, BATCH, H, NOPE + ROPE)
    group_cache = latent_cache.reshape(N_REP, RES, CTX, KV + ROPE)
    key_weight = key_absorb.astype(jnp.float32)
    value_matrix = value_head_projection.astype(jnp.float32)

    def one_group(bundle):
        queries, caches, anchor = bundle
        absorbed = jnp.einsum('thn,hnk->thk', queries[:, :, :NOPE].astype(jnp.float32), key_weight).astype(jnp.bfloat16)
        joined = jnp.concatenate([absorbed, queries[:, :, NOPE:]], axis=2)
        near_scores = jnp.einsum('ihk,ipk->ihp', joined[:RES].astype(jnp.float32), caches.astype(jnp.float32)) * scaling_factor
        latent_near = jnp.einsum('ihp,ipk->ihk', normalize(near_scores).astype(jnp.float32), caches[:, :, :KV].astype(jnp.float32)).astype(jnp.bfloat16)
        mig_rows = lax.dynamic_index_in_dim(moved_rows, anchor, 0, keepdims=False)
        length = lax.dynamic_index_in_dim(moved_length, anchor, 0, keepdims=False)
        far_scores = jnp.dot(joined[RES], mig_rows.T, preferred_element_type=jnp.float32) * scaling_factor
        usable = jnp.arange(MIGLEN, dtype=jnp.int32) < length
        far_scores = jnp.where(usable[None, :], far_scores, -1e+30)
        latent_far = jnp.dot(normalize(far_scores), mig_rows[:, :KV], preferred_element_type=jnp.float32).astype(jnp.bfloat16)
        latent_vectors = jnp.concatenate([latent_near, latent_far[None]], axis=0)
        return jnp.einsum('ygf,gfw->ygw', latent_vectors.astype(jnp.float32), value_matrix).astype(jnp.bfloat16)
    head_out = lax.map(one_group, (group_query, group_cache, source))
    attended = jnp.dot(head_out.reshape(TOKENS, H * VD), out_proj, preferred_element_type=jnp.float32)
    combined = residual.astype(jnp.float32) + attended
    scaled = combined * norm_gain.astype(jnp.float32)[None, :]
    root_mean = jnp.sqrt(lax.optimization_barrier(jnp.mean(combined * combined, axis=1, keepdims=True)) + 1e-06)
    normed = (scaled / root_mean).astype(jnp.bfloat16)
    logit_table = jnp.dot(scaled, centroid.astype(jnp.float32).T, precision=lax.Precision.HIGHEST)
    router_logit = jnp.take_along_axis(logit_table, expert_ids, axis=1) / root_mean
    affinity = jax.nn.sigmoid(router_logit)
    weight_share = 2.5 * affinity / lax.optimization_barrier(jnp.sum(affinity, axis=1, keepdims=True))
    pair_expert, pair_slot = expert_slots(expert_ids, EXPERTS)
    slot_token = jnp.zeros((EXPERTS, CAP), jnp.int32).at[pair_expert, pair_slot].set(jnp.arange(TOKENS * TOPK, dtype=jnp.int32) // TOPK)

    def one_expert(bundle):
        chosen, up_proj, down_proj = bundle
        expert_rows = normed[chosen]
        hidden = jax.nn.silu(jnp.dot(expert_rows, up_proj, preferred_element_type=jnp.float32)).astype(jnp.bfloat16)
        return jnp.dot(hidden, down_proj, preferred_element_type=jnp.float32).astype(jnp.bfloat16)
    served = lax.map(one_expert, (slot_token, up_weight, down_weight))
    returned_rows = served[pair_expert, pair_slot].astype(jnp.float32).reshape(TOKENS, TOPK, D)
    routed_expert_sum = lax.optimization_barrier(jnp.sum(weight_share[:, :, None] * returned_rows, axis=1))
    return (combined + routed_expert_sum).astype(jnp.bfloat16)
```

```python
import functools
import math
import types

import jax
import jax.numpy as jnp
from jax import lax
from jax.experimental import pallas as pl
from jax.experimental.pallas import tpu as pltpu
from jax.sharding import PartitionSpec as P

MESH = pl.DeviceIdType.MESH
F32 = jnp.float32
BF16 = jnp.bfloat16
RES = 8
SLOTS = 40
CORES = 2


def nn(a, b):
    return lax.dot_general(a, b, (((1,), (0,)), ((), ())), preferred_element_type=F32)


def nt(a, b):
    return lax.dot_general(a, b, (((1,), (1,)), ((), ())), preferred_element_type=F32)


def one_hot(mask):
    return jnp.where(mask, 1.0, 0.0).astype(BF16)


def iota(shape, dim):
    return lax.broadcasted_iota(jnp.int32, shape, dim)


def split2(value):
    high = value.astype(BF16).astype(F32)
    return high, (value - high).astype(BF16).astype(F32)


def layer_kernel(names, dims, *refs):
    (
        source_ref, length_ref, query_hbm, cache_hbm, moved_hbm, absorb_hbm, value_hbm, outproj_hbm,
        residual_hbm, gain_hbm, centroid_hbm, ids_hbm, up_hbm, down_hbm, out_ref,
    ) = refs[:15]
    s = types.SimpleNamespace(**dict(zip(names, refs[15:])))
    reps, heads, lines, xs, zs, groups, moved_n, columns, tokens, features = dims
    line_columns = columns * CORES * heads
    width = -(-line_columns // 128) * 128
    pitch = -(-columns // 16) * 16
    batch = tokens // reps
    half = lines * batch
    head_rows = batch * 16
    kv = value_hbm.shape[1]
    nope = absorb_hbm.shape[1]
    qdim = query_hbm.shape[1]
    rope = qdim - nope
    full = kv + rope
    head_features = 16 * value_hbm.shape[2]
    scale = 1.0 / math.sqrt(qdim)

    rep = lax.axis_index("rep")
    head = lax.axis_index("head")
    line = rep // CORES
    core = rep % CORES
    lx = line // zs
    lz = line % zs
    owner = core * heads + head

    def rep_at(dx, dz, dc):
        return (((lx + dx) % xs) * zs + (lz + dz) % zs) * CORES + (core + dc) % CORES

    def line_at(dx, dz):
        return ((lx + dx) % xs) * zs + (lz + dz) % zs

    line_offsets = [(dx, dz) for dx in range(xs) for dz in range(zs) if (dx, dz) != (0, 0)]
    line_offsets.sort(key=lambda o: -(min(o[0], xs - o[0]) + min(o[1], zs - o[1])))
    plane_offsets = [(dx, dz, dc) for dx, dz in line_offsets for dc in range(CORES)]
    plane_offsets += [(0, 0, dc) for dc in range(1, CORES)]

    def load(src, dst, sem):
        copy = pltpu.make_async_copy(src, dst, s.load_sem.at[sem])
        copy.start()
        return copy

    load_moved = load(moved_hbm, s.moved, 0)
    load_query = load(query_hbm, s.query, 1)
    load_absorb = load(absorb_hbm, s.absorb, 2)
    load_outproj = load(outproj_hbm, s.outproj, 3)
    load_residual = load(residual_hbm, s.residual, 4)
    load_gain = load(gain_hbm, s.gain, 5)
    load_centroid = load(centroid_hbm, s.centroid, 6)
    load_ids = load(ids_hbm, s.ids, 7)
    load_cache = load(cache_hbm, s.cache, 8)
    load_value = load(value_hbm, s.value, 9)
    load_up = load(up_hbm, s.up, 10)
    chunk = zs * line_columns
    load_down = [load(down_hbm.at[:, pl.ds(i * chunk, chunk)], s.down.at[i], 11 + i) for i in range(xs)]

    barrier = pltpu.get_barrier_semaphore()
    partners = [(rep_at(*o), head) for o in plane_offsets]
    for dh in range(1, heads):
        for dc in range(CORES):
            partners.append((rep_at(0, 0, dc), (head + dh) % heads))
    for partner in partners:
        pl.semaphore_signal(barrier, inc=1, device_id=partner, device_id_type=MESH)

    load_moved.wait()
    for g in range(groups):
        s.moved_out[g] = s.moved[source_ref[g]]
    s.moved_in[rep] = s.moved_out[rep]

    load_outproj.wait()
    pad = jnp.zeros((pitch - columns, 512), F32)
    for i in range(outproj_hbm.shape[1] // 512):
        cut = s.outproj[:, pl.ds(512 * i, 512)].astype(F32)
        s.cols_out[:, pl.ds(512 * i, 512)] = jnp.concatenate([cut, pad], axis=0).astype(BF16)
    for copy in (load_residual, load_gain, load_centroid, load_ids):
        copy.wait()
    tok_lanes = -(-tokens // 128) * 128
    experts = centroid_hbm.shape[1]
    exp_lanes = -(-experts // 128) * 128
    s.static_out[...] = jnp.zeros_like(s.static_out)

    def padded(value):
        return jnp.concatenate([value.astype(F32), jnp.zeros((pitch - columns, value.shape[1]), F32)], axis=0).astype(BF16)

    s.static_out[:, pl.ds(0, tokens)] = padded(s.residual[...])
    s.static_out[:, pl.ds(tok_lanes, experts)] = padded(s.centroid[...])
    gain_row = jnp.broadcast_to(s.gain[...].astype(F32), (pitch, columns))
    diagonal = iota((pitch, columns), 0) == iota((pitch, columns), 1)
    gain_col = jnp.sum(jnp.where(diagonal, gain_row, 0.0), axis=1, keepdims=True)
    first_lane = iota((pitch, 128), 1) == 0
    s.static_out[:, pl.ds(tok_lanes + exp_lanes, 128)] = jnp.where(first_lane, gain_col, 0.0).astype(BF16)

    pl.semaphore_wait(barrier, len(partners))

    def push(src, dst, phase, k, to_rep, to_head):
        copy = pltpu.make_async_remote_copy(
            src_ref=src, dst_ref=dst, send_sem=phase.at[0, k], recv_sem=phase.at[1, k],
            device_id=(to_rep, to_head), device_id_type=MESH,
        )
        copy.start()
        return copy

    started = []
    rows_copies = []
    for k, offset in enumerate(plane_offsets):
        to_rep = rep_at(*offset)
        rows_copies.append(push(s.moved_out.at[to_rep], s.moved_in.at[rep], s.rows_sem, k, to_rep, head))

    own_rows = pl.ds(pl.multiple_of(owner * pitch, pitch), pitch)
    cols_copies = []
    static_copies = []
    for dh in range(1, heads):
        to_head = (head + dh) % heads
        lanes = pl.ds(pl.multiple_of(to_head * head_features, 128), head_features)
        cols_copies.append(push(s.cols_out.at[:, lanes], s.cols_in.at[own_rows], s.cols_sem, dh - 1, rep, to_head))
        static_copies.append(push(s.static_out, s.static_in.at[own_rows], s.static_sem, dh - 1, rep, to_head))
    own_lanes = pl.ds(pl.multiple_of(head * head_features, 128), head_features)
    own_cols = pltpu.make_async_copy(s.cols_out.at[:, own_lanes], s.cols_in.at[own_rows], s.load_sem.at[11 + xs])
    own_cols.start()
    own_static = pltpu.make_async_copy(s.static_out, s.static_in.at[own_rows], s.load_sem.at[12 + xs])
    own_static.start()

    load_query.wait()
    s.query_f[...] = s.query[:, pl.ds(0, nope)].astype(F32)
    s.joined[kv // 128, :, pl.ds(0, rope)] = s.query[:, pl.ds(nope, rope)].astype(F32)
    load_absorb.wait()
    for h in range(16):
        part = s.query_f[pl.ds(h, batch, stride=16), :].astype(BF16)
        absorbed = nn(part, s.absorb[h])
        for i in range(kv // 128):
            s.joined[i, pl.ds(h, batch, stride=16), :] = absorbed[:, 128 * i:128 * i + 128]

    def joined_query(i):
        parts = [s.joined[j, pl.ds(16 * i, 16), :] for j in range(kv // 128)]
        parts.append(s.joined[kv // 128, pl.ds(16 * i, 16), pl.ds(0, rope)])
        return jnp.concatenate(parts, axis=1).astype(BF16)

    def keep_latents(i, value):
        for j in range(kv // 128):
            s.latents[j, pl.ds(16 * i, 16), :] = value[:, 128 * j:128 * j + 128]

    s.far_query[...] = joined_query(RES)
    query_copies = []
    for dh in range(1, heads):
        query_copies.append(push(s.far_query, s.far_queries.at[head], s.query_sem, dh - 1, rep, (head + dh) % heads))
    s.far_queries[head] = s.far_query[...]

    load_cache.wait()
    for i in range(RES):
        scores = nn(joined_query(i), s.cache[i]) * scale
        weights = jnp.exp(scores - jnp.max(scores, axis=1, keepdims=True))
        weights = (weights / jnp.sum(weights, axis=1, keepdims=True)).astype(BF16)
        keep_latents(i, nt(weights, s.cache[i, pl.ds(0, kv), :]))

    for copy in cols_copies + static_copies:
        copy.wait_recv()
    own_cols.wait()
    own_static.wait()
    core_rows = pl.ds(pl.multiple_of(core * (heads * pitch), heads * pitch), heads * pitch)
    other = rep_at(0, 0, 1)
    cols_pass = push(s.cols_in.at[core_rows], s.cols_in.at[core_rows], s.cols_sem, heads - 1, other, head)
    static_pass = push(s.static_in.at[core_rows], s.static_in.at[core_rows], s.static_sem, heads - 1, other, head)

    row_count = reps * moved_n
    s.rows_f[pl.ds(pl.multiple_of(rep * moved_n, moved_n), moved_n), :] = s.moved_in[rep].astype(F32)
    for copy, (dx, dz, dc) in zip(rows_copies, plane_offsets):
        copy.wait_recv()
        from_rep = rep_at(-dx, -dz, -dc)
        s.rows_f[pl.ds(pl.multiple_of(from_rep * moved_n, moved_n), moved_n), :] = s.moved_in[from_rep].astype(F32)
    s.rows_b[...] = s.rows_f[...].astype(BF16)
    for copy in query_copies:
        copy.wait_recv()
    far_all = jnp.concatenate([s.far_queries[h] for h in range(heads)], axis=0)
    far_scores = nt(far_all, s.rows_b[...]) * scale
    place = iota((1, row_count), 1)
    from_device = (place * 2731) >> 16
    position = place + from_device * (moved_n * (heads - 1)) + head * moved_n
    far_scores = jnp.where(position < length_ref[rep], far_scores, -1e30)
    far_max = jnp.max(far_scores, axis=1, keepdims=True)
    far_weights = jnp.exp(far_scores - far_max)
    far_sum = jnp.sum(far_weights, axis=1, keepdims=True)
    s.far_out[:, pl.ds(0, kv)] = nn(far_weights.astype(BF16), s.rows_b[:, pl.ds(0, kv)])
    lane = iota((heads * 16, 128), 1)
    s.far_out[:, pl.ds(kv, 128)] = jnp.where(lane == 0, far_max, jnp.where(lane == 1, far_sum, 0.0))
    far_copies = []
    for dh in range(1, heads):
        to_head = (head + dh) % heads
        their_rows = pl.ds(pl.multiple_of(to_head * 16, 16), 16)
        far_copies.append(push(s.far_out.at[their_rows], s.far_in.at[head], s.far_sem, dh - 1, rep, to_head))
    s.far_in[head] = s.far_out[pl.ds(pl.multiple_of(head * 16, 16), 16), :]
    load_value.wait()
    for copy in far_copies:
        copy.wait_recv()
    top = s.far_in[0, :, pl.ds(kv, 1)]
    for h in range(1, heads):
        top = jnp.maximum(top, s.far_in[h, :, pl.ds(kv, 1)])
    total = jnp.zeros((16, kv), F32)
    weight_sum = jnp.zeros((16, 1), F32)
    for h in range(heads):
        factor = jnp.exp(s.far_in[h, :, pl.ds(kv, 1)] - top)
        total = total + factor * s.far_in[h, :, pl.ds(0, kv)]
        weight_sum = weight_sum + factor * s.far_in[h, :, pl.ds(kv + 1, 1)]
    keep_latents(RES, total / weight_sum)

    for h in range(16):
        parts = [s.latents[i, pl.ds(h, batch, stride=16), :] for i in range(kv // 128)]
        part = jnp.concatenate(parts, axis=1).astype(BF16)
        s.heads_f[pl.ds(h, batch, stride=16), :] = nn(part, s.value[h])
    s.heads_out[...] = s.heads_f[...].astype(BF16)
    head_copies = []
    for k, (dx, dz) in enumerate(line_offsets):
        head_copies.append(push(s.heads_out, s.heads_in.at[line], s.heads_sem, k, rep_at(dx, dz, 0), head))
    s.heads_in[line] = s.heads_out[...]

    cols_pass.wait_recv()
    static_pass.wait_recv()
    row = iota((width, width), 0)
    col = iota((width, width), 1)
    squeeze = one_hot((row < line_columns) & (col == row + (pitch - columns) * ((row * 2341) >> 16)))
    for i in range(head_features // 512):
        cut = pl.ds(512 * i, 512)
        s.cols[:, cut] = nn(squeeze, s.cols_in[:, cut]).astype(BF16)
    static = nn(squeeze, s.static_in[...]).astype(BF16)
    held = iota((tokens, tokens), 0)
    held_core = jnp.where(held >= half, 1, 0)
    held_line = ((held - half * held_core) * 7282) >> 16
    order = held - half * held_core + batch * (held_line + held_core)
    reorder = one_hot(iota((tokens, tokens), 1) == order)
    s.reorder[...] = reorder
    s.residual_c[...] = nt(reorder, static[:, :tokens])
    their_expert = iota((lines, experts), 0) * (CORES * heads) + owner
    pick = one_hot(iota((lines, experts), 1) == their_expert)
    s.centroid_c[...] = nt(pick, static[:, tok_lanes:tok_lanes + experts])
    first = one_hot((iota((8, 128), 0) == 0) & (iota((8, 128), 1) == 0))
    s.gain_c[...] = nt(first, static[:, tok_lanes + exp_lanes:])
    named = jnp.zeros((lines, tokens), F32)
    my_experts = iota((lines, tokens), 0) * (CORES * heads) + owner
    for k in range(ids_hbm.shape[0]):
        named = jnp.where(my_experts == s.ids[pl.ds(k, 1), :], 1.0, named)
    earlier = one_hot(iota((tokens, tokens), 0) < iota((tokens, tokens), 1))
    slot = jnp.where(named > 0.0, nn(named.astype(BF16), earlier), -1.0)
    slot_index = iota((SLOTS, tokens), 0).astype(F32)
    pieces = [jnp.where(slot[e:e + 1, :] == slot_index, 1.0, 0.0) for e in range(lines)]
    s.gather[...] = jnp.concatenate(pieces, axis=0).astype(BF16)
    s.gather_held[...] = nt(s.gather[...], reorder).astype(BF16)
    eye = one_hot(iota((tokens, tokens), 0) == iota((tokens, tokens), 1))
    s.scatter[...] = nt(eye, s.gather[...]).astype(BF16)

    s.heads_w[pl.ds(pl.multiple_of(line * head_rows, head_rows), head_rows), :] = s.heads_in[line].astype(F32)
    for copy, (dx, dz) in zip(head_copies, line_offsets):
        copy.wait_recv()
        from_line = line_at(-dx, -dz)
        s.heads_w[pl.ds(pl.multiple_of(from_line * head_rows, head_rows), head_rows), :] = s.heads_in[from_line].astype(F32)
    acts = [s.heads_w[pl.ds(h, half, stride=16), :].astype(BF16) for h in range(16)]
    partial = nt(jnp.concatenate(acts, axis=1), s.cols[...])
    s.sum_out[...] = partial.astype(BF16)
    sum_copies = []
    for dh in range(1, heads):
        sum_copies.append(push(s.sum_out, s.sum_in.at[dh - 1], s.sum_sem, dh - 1, rep, (head + dh) % heads))
    for dh, copy in enumerate(sum_copies):
        copy.wait_recv()
        partial = partial + s.sum_in[dh].astype(F32)
    s.swap_out[...] = partial
    swap = push(s.swap_out, s.swap_in, s.swap_sem, 0, other, head)
    swap.wait_recv()
    mine, theirs = s.swap_out[...], s.swap_in[...]
    first_core = core == 0
    attended = jnp.concatenate([jnp.where(first_core, mine, theirs), jnp.where(first_core, theirs, mine)], axis=0)
    combined = s.residual_c[...] + attended
    s.combined[...] = combined

    square_high, square_low = split2(jnp.sum(combined * combined, axis=1, keepdims=True))
    scaled = combined * s.gain_c[0:1, :]
    token_lane = iota((tokens, width), 1)
    scaled = jnp.where(token_lane == line_columns, square_high, scaled)
    scaled = jnp.where(token_lane == line_columns + 1, square_low, scaled)
    gathered = nn(s.gather_held[...], scaled.astype(BF16))
    slot_lane = iota((SLOTS, width), 1)
    for e in range(lines):
        rows = gathered[SLOTS * e:SLOTS * e + SLOTS]
        high, low = split2(jnp.sum(rows * s.centroid_c[e:e + 1, :], axis=1, keepdims=True))
        rows = jnp.where(slot_lane == line_columns + 2, high, rows)
        rows = jnp.where(slot_lane == line_columns + 3, low, rows)
        s.tok_out[e] = rows.astype(BF16)
    tok_copies = []
    for k, (dx, dz) in enumerate(line_offsets):
        tok_copies.append(push(s.tok_out.at[line_at(dx, dz)], s.tok_in.at[line], s.tok_sem, k, rep_at(dx, dz, 0), head))
    s.tok_in[line] = s.tok_out[line]

    rest = combined
    my_columns = one_hot((iota((pitch, width), 0) < columns) & (iota((pitch, width), 1) == owner * columns + iota((pitch, width), 0)))
    combined_own = jnp.zeros((pitch, tokens), F32)
    for _ in range(3):
        part = rest.astype(BF16)
        rest = rest - part.astype(F32)
        combined_own = combined_own + nn(nt(my_columns, part).astype(BF16), s.reorder[...])
    s.combined_own[...] = combined_own

    load_up.wait()
    inner = nn(s.tok_in[line][:, :line_columns], s.up[line])
    stats = s.tok_in[line].astype(F32)[:, width - 128:]
    for copy, (dx, dz) in zip(tok_copies, line_offsets):
        copy.wait_recv()
        from_line = line_at(-dx, -dz)
        rows = s.tok_in[from_line]
        inner = inner + nn(rows[:, :line_columns], s.up[from_line])
        stats = stats + rows.astype(F32)[:, width - 128:]
    at = line_columns - (width - 128)
    squares = stats[:, at:at + 1] + stats[:, at + 1:at + 2]
    logit = stats[:, at + 2:at + 3] + stats[:, at + 3:at + 4]
    root_mean = jnp.sqrt(squares / features + 1e-6)
    inner = inner / root_mean
    hidden = (inner * jax.nn.sigmoid(inner)).astype(BF16)
    affinity = jax.nn.sigmoid(logit / root_mean)
    affinity_high, affinity_low = split2(affinity)
    for copy in load_down:
        copy.wait()
    back_copies = []
    filler = jnp.zeros((SLOTS, width - line_columns), F32)
    x_order = sorted(range(xs), key=lambda dx: -min(dx, xs - dx))
    for dx in x_order:
        to_x = (lx + dx) % xs
        result = nn(hidden, s.down[to_x]) * affinity
        for z in range(zs):
            piece = jnp.concatenate([result[:, z * line_columns:(z + 1) * line_columns], filler], axis=1)
            piece = jnp.where(slot_lane == line_columns, affinity_high, piece)
            piece = jnp.where(slot_lane == line_columns + 1, affinity_low, piece)
            s.back_out[to_x * zs + z] = piece.astype(BF16)
        for dz in range(zs):
            if (dx, dz) != (0, 0):
                k = line_offsets.index((dx, dz))
                back_copies.append((k, push(s.back_out.at[line_at(dx, dz)], s.back_in.at[line], s.back_sem, k, rep_at(dx, dz, 0), head)))
    s.back_in[line] = s.back_out[line]
    for _, copy in back_copies:
        copy.wait_recv()

    returned = jnp.concatenate([s.back_in[e].astype(F32) for e in range(lines)], axis=0).astype(BF16)
    summed = nn(s.scatter[...], returned)
    share_high, share_low = split2(summed[:, line_columns:line_columns + 1] + summed[:, line_columns + 1:line_columns + 2])
    summed = jnp.where(token_lane == line_columns, share_high, summed)
    summed = jnp.where(token_lane == line_columns + 1, share_low, summed)
    place_in = row & (pitch - 1)
    wanted = jnp.where(place_in < columns, row - (pitch - columns) * (row // pitch), line_columns + place_in - columns)
    spread = one_hot((col == wanted) & (place_in < columns + 2))
    pieces = nt(spread, summed.astype(BF16)).astype(BF16)
    for j in range(CORES * heads):
        s.last_out[j] = pieces[pitch * j:pitch * j + pitch]
    last_copies = []
    k = 0
    for dc in range(CORES):
        for dh in range(heads):
            if (dc, dh) != (0, 0):
                to_core, to_head = (core + dc) % CORES, (head + dh) % heads
                last_copies.append(push(
                    s.last_out.at[to_core * heads + to_head], s.last_in.at[owner], s.last_sem, k, rep_at(0, 0, dc), to_head))
                k += 1
    s.last_in[owner] = s.last_out[owner]
    for copy in last_copies:
        copy.wait_recv()
    routed = s.last_in[0].astype(F32)
    for j in range(1, CORES * heads):
        routed = routed + s.last_in[j].astype(F32)
    share = routed[columns:columns + 1] + routed[columns + 1:columns + 2]
    layer_out = s.combined_own[...] + 2.5 * routed / share
    out_ref[...] = layer_out[:columns].astype(BF16)

    sends = rows_copies + cols_copies + static_copies + [cols_pass, static_pass] + query_copies + far_copies
    sends += head_copies + sum_copies + [swap] + tok_copies + [copy for _, copy in back_copies] + last_copies
    for copy in sends:
        copy.wait_send()


def per_device(
    query, latent_cache, moved_rows, target_group, moved_length, key_absorb, value_head_projection,
    out_proj, residual, norm_gain, centroid, expert_ids, up_weight, down_weight,
):
    reps = lax.axis_size("rep")
    heads = lax.axis_size("head")
    lines = reps // CORES
    xs = 4 if lines % 4 == 0 else lines
    zs = lines // xs
    groups, moved_n, full = moved_rows.shape
    batch, local_heads, qdim = query.shape
    columns = out_proj.shape[1]
    tokens, topk = expert_ids.shape
    features, hidden = up_weight.shape[1:]
    experts = centroid.shape[0]
    kv = value_head_projection.shape[1]
    vd = value_head_projection.shape[2]
    context = latent_cache.shape[1]
    line_columns = columns * CORES * heads
    width = -(-line_columns // 128) * 128
    pitch = -(-columns // 16) * 16
    half = tokens // CORES
    tok_lanes = -(-tokens // 128) * 128
    static_lanes = tok_lanes + -(-experts // 128) * 128 + 128
    head_features = local_heads * vd

    match = target_group[None, :] == jnp.arange(groups, dtype=jnp.int32)[:, None]
    source = jnp.sum(jnp.where(match, jnp.arange(groups, dtype=jnp.int32)[None, :], 0), axis=1)
    length = jnp.sum(jnp.where(match, moved_length[None, :], 0), axis=1)

    vmem = dict(
        moved=((groups, moved_n, full), BF16),
        moved_out=((groups, moved_n, full), BF16),
        moved_in=((reps, moved_n, full), BF16),
        rows_f=((reps * moved_n, full), F32),
        rows_b=((reps * moved_n, full), BF16),
        query=((batch * local_heads, qdim), BF16),
        query_f=((batch * local_heads, 128), F32),
        absorb=(key_absorb.shape, BF16),
        value=(value_head_projection.shape, BF16),
        cache=((latent_cache.shape[0], full, context), BF16),
        outproj=((columns, out_proj.shape[0]), BF16),
        cols_out=((pitch, out_proj.shape[0]), BF16),
        cols_in=((pitch * CORES * heads, head_features), BF16),
        cols=((width, head_features), BF16),
        residual=((columns, tokens), BF16),
        gain=((1, columns), BF16),
        centroid=((columns, experts), BF16),
        ids=((topk, tokens), jnp.int32),
        static_out=((pitch, static_lanes), BF16),
        static_in=((pitch * CORES * heads, static_lanes), BF16),
        residual_c=((tokens, width), F32),
        centroid_c=((lines, width), F32),
        gain_c=((8, width), F32),
        reorder=((tokens, tokens), BF16),
        gather=((lines * SLOTS, tokens), BF16),
        gather_held=((lines * SLOTS, tokens), BF16),
        scatter=((tokens, lines * SLOTS), BF16),
        joined=((kv // 128 + 1, batch * local_heads, 128), F32),
        latents=((kv // 128, batch * local_heads, 128), F32),
        heads_f=((batch * local_heads, vd), F32),
        heads_out=((batch * local_heads, vd), BF16),
        heads_in=((lines, batch * local_heads, vd), BF16),
        heads_w=((lines * batch * local_heads, vd), F32),
        far_query=((local_heads, full), BF16),
        far_queries=((heads, local_heads, full), BF16),
        far_out=((heads * local_heads, kv + 128), F32),
        far_in=((heads, local_heads, kv + 128), F32),
        sum_out=((half, width), BF16),
        sum_in=((heads - 1, half, width), BF16),
        swap_out=((half, width), F32),
        swap_in=((half, width), F32),
        combined=((tokens, width), F32),
        combined_own=((pitch, tokens), F32),
        tok_out=((lines, SLOTS, width), BF16),
        tok_in=((lines, SLOTS, width), BF16),
        up=((lines, line_columns, hidden), BF16),
        down=((xs, hidden, zs * line_columns), BF16),
        back_out=((lines, SLOTS, width), BF16),
        back_in=((lines, SLOTS, width), BF16),
        last_out=((CORES * heads, pitch, tokens), BF16),
        last_in=((CORES * heads, pitch, tokens), BF16),
    )
    sems = dict(
        load_sem=(13 + xs,), rows_sem=(2, reps - 1), cols_sem=(2, heads), static_sem=(2, heads),
        query_sem=(2, heads - 1), far_sem=(2, heads - 1), heads_sem=(2, lines - 1), sum_sem=(2, heads - 1),
        swap_sem=(2, 1), tok_sem=(2, lines - 1), back_sem=(2, lines - 1), last_sem=(2, CORES * heads - 1),
    )
    names = list(vmem) + list(sems)
    scratch = [pltpu.VMEM(shape, dtype) for shape, dtype in vmem.values()]
    scratch += [pltpu.SemaphoreType.DMA(shape) for shape in sems.values()]
    dims = (reps, heads, lines, xs, zs, groups, moved_n, columns, tokens, features)
    layer_out = pl.pallas_call(
        functools.partial(layer_kernel, names, dims),
        out_shape=jax.ShapeDtypeStruct((columns, tokens), BF16),
        in_specs=[pl.BlockSpec(memory_space=pltpu.SMEM)] * 2 + [pl.BlockSpec(memory_space=pl.ANY)] * 12,
        out_specs=pl.BlockSpec(memory_space=pltpu.VMEM),
        scratch_shapes=scratch,
        compiler_params=pltpu.CompilerParams(
            collective_id=0, has_side_effects=True, vmem_limit_bytes=60 * 1024 * 1024
        ),
        name="latent_moe_layer",
    )(
        source, length, query.reshape(batch * local_heads, qdim), jnp.swapaxes(latent_cache, 1, 2), moved_rows,
        key_absorb, value_head_projection, out_proj.T, residual.T, norm_gain.reshape(1, columns), centroid.T,
        expert_ids.T, up_weight.reshape(lines, line_columns, hidden), down_weight[0],
    )
    return layer_out.T


def solution(mesh):
    return jax.shard_map(
        per_device,
        mesh=mesh,
        in_specs=(
            P("rep", "head", None),
            P("rep", None, None),
            P(None, ("rep", "head"), None),
            P(),
            P(),
            P("head", None, None),
            P("head", None, None),
            P(None, ("rep", "head")),
            P(None, ("rep", "head")),
            P(("rep", "head")),
            P(None, ("rep", "head")),
            P(),
            P(("rep", "head"), None, None),
            P(("rep", "head"), None, None),
        ),
        out_specs=P(None, ("rep", "head")),
        check_vma=False,
    )
```

```python
import functools
import math
import types

import jax
import jax.numpy as jnp
from jax import lax
from jax.experimental import pallas as pl
from jax.experimental.pallas import tpu as pltpu
from jax.sharding import PartitionSpec as P

MESH = pl.DeviceIdType.MESH
F32 = jnp.float32
BF16 = jnp.bfloat16
RES = 8
SLOTS = 40
CORES = 2


def nn(a, b):
    return lax.dot_general(a, b, (((1,), (0,)), ((), ())), preferred_element_type=F32)


def nt(a, b):
    return lax.dot_general(a, b, (((1,), (1,)), ((), ())), preferred_element_type=F32)


def one_hot(mask):
    return jnp.where(mask, 1.0, 0.0).astype(BF16)


def iota(shape, dim):
    return lax.broadcasted_iota(jnp.int32, shape, dim)


def split2(value):
    high = value.astype(BF16).astype(F32)
    return high, (value - high).astype(BF16).astype(F32)


def layer_kernel(names, dims, *refs):
    (
        target_hbm, length_hbm, query_hbm, cache_hbm, moved_hbm, absorb_hbm, value_hbm, outproj_hbm,
        residual_hbm, gain_hbm, centroid_hbm, ids_hbm, up_hbm, down_hbm, out_ref,
    ) = refs[:15]
    s = types.SimpleNamespace(**dict(zip(names, refs[15:])))
    reps, heads, lines, xs, zs, groups, moved_n, columns, tokens, features = dims
    line_columns = columns * CORES * heads
    width = -(-line_columns // 128) * 128
    pitch = -(-columns // 16) * 16
    batch = tokens // reps
    half = lines * batch
    near = lines * RES
    kv = value_hbm.shape[1]
    nope = absorb_hbm.shape[1]
    qdim = query_hbm.shape[1]
    rope = qdim - nope
    full = kv + rope
    head_features = 16 * value_hbm.shape[2]
    scale = 1.0 / math.sqrt(qdim)

    rep = lax.axis_index("rep")
    head = lax.axis_index("head")
    line = rep // CORES
    core = rep % CORES
    lx = line // zs
    lz = line % zs
    owner = core * heads + head

    def rep_at(dx, dz, dc):
        return (((lx + dx) % xs) * zs + (lz + dz) % zs) * CORES + (core + dc) % CORES

    def line_at(dx, dz):
        return ((lx + dx) % xs) * zs + (lz + dz) % zs

    line_offsets = [(dx, dz) for dx in range(xs) for dz in range(zs) if (dx, dz) != (0, 0)]
    line_offsets.sort(key=lambda o: -(min(o[0], xs - o[0]) + min(o[1], zs - o[1])))
    plane_offsets = [(dx, dz, dc) for dx, dz in line_offsets for dc in range(CORES)]
    plane_offsets += [(0, 0, dc) for dc in range(1, CORES)]

    line_places = [(dc, dh) for dc in range(CORES) for dh in range(heads) if (dc, dh) != (0, 0)]

    def load(src, dst, sem):
        copy = pltpu.make_async_copy(src, dst, s.load_sem.at[sem])
        copy.start()
        return copy

    load_target = load(target_hbm, s.target, 0)
    load_length = load(length_hbm, s.length, 1)
    load_moved = load(moved_hbm, s.moved, 2)

    barrier = pltpu.get_barrier_semaphore()
    partners = [(rep_at(*o), head) for o in plane_offsets]
    for dh in range(1, heads):
        for dc in range(CORES):
            partners.append((rep_at(0, 0, dc), (head + dh) % heads))
    for partner in partners:
        pl.semaphore_signal(barrier, inc=1, device_id=partner, device_id_type=MESH)
    load_query = load(query_hbm, s.query, 3)
    load_absorb = load(absorb_hbm, s.absorb, 4)
    load_cache = load(cache_hbm, s.cache, 5)
    load_ids = load(ids_hbm, s.ids, 6)
    load_residual = load(residual_hbm, s.residual, 7)
    load_gain = load(gain_hbm, s.gain, 8)
    load_centroid = load(centroid_hbm, s.centroid, 9)
    load_outproj = load(outproj_hbm, s.outproj, 10)
    load_value = load(value_hbm, s.value, 11)

    load_target.wait()
    load_length.wait()
    matches = iota((groups, groups), 0) == s.target[...]
    source = jnp.sum(jnp.where(matches, iota((groups, groups), 1), 0), axis=1, keepdims=True)
    s.source_v[...] = jnp.broadcast_to(source, (groups, 128))
    load_source = load(s.source_v, s.source_s, 12)
    my_match = matches & (iota((groups, groups), 0) == rep)
    length = jnp.sum(jnp.sum(jnp.where(my_match, s.length[...], 0), axis=1, keepdims=True), axis=0, keepdims=True)
    load_source.wait()
    load_moved.wait()
    for g in range(groups):
        s.moved_out[g] = s.moved[jnp.clip(s.source_s[g, 0], 0, groups - 1)]


    pl.semaphore_wait(barrier, len(partners))

    def push(src, dst, phase, k, to_rep, to_head):
        copy = pltpu.make_async_remote_copy(
            src_ref=src, dst_ref=dst, send_sem=phase.at[0, k], recv_sem=phase.at[1, k],
            device_id=(to_rep, to_head), device_id_type=MESH,
        )
        copy.start()
        return copy

    rows_copies = []
    for k, offset in enumerate(plane_offsets):
        to_rep = rep_at(*offset)
        rows_copies.append(push(s.moved_out.at[to_rep], s.moved_in.at[rep], s.rows_sem, k, to_rep, head))

    load_query.wait()
    s.query_f[...] = s.query[:, pl.ds(0, nope)].astype(F32)
    s.joined[kv // 128, :, pl.ds(0, rope)] = s.query[:, pl.ds(nope, rope)].astype(F32)
    load_absorb.wait()
    for h in range(16):
        part = s.query_f[pl.ds(h, batch, stride=16), :].astype(BF16)
        absorbed = nn(part, s.absorb[h])
        for i in range(kv // 128):
            s.joined[i, pl.ds(h, batch, stride=16), :] = absorbed[:, 128 * i:128 * i + 128]

    def joined_query(i):
        parts = [s.joined[j, pl.ds(16 * i, 16), :] for j in range(kv // 128)]
        parts.append(s.joined[kv // 128, pl.ds(16 * i, 16), pl.ds(0, rope)])
        return jnp.concatenate(parts, axis=1).astype(BF16)

    def keep_latents(i, value):
        for j in range(kv // 128):
            s.latents[j, pl.ds(16 * i, 16), :] = value[:, 128 * j:128 * j + 128]

    s.far_query[...] = joined_query(RES)
    query_copies = []
    for dh in range(1, heads):
        query_copies.append(push(s.far_query, s.far_queries.at[head], s.query_sem, dh - 1, rep, (head + dh) % heads))
    s.far_queries[head] = s.far_query[...]

    load_outproj.wait()
    pad = jnp.zeros((pitch - columns, 512), F32)
    for i in range(outproj_hbm.shape[1] // 512):
        cut = s.outproj[:, pl.ds(512 * i, 512)].astype(F32)
        s.cols_out[:, pl.ds(512 * i, 512)] = jnp.concatenate([cut, pad], axis=0).astype(BF16)
    for copy in (load_residual, load_gain, load_centroid, load_ids):
        copy.wait()
    tok_lanes = -(-tokens // 128) * 128
    experts = centroid_hbm.shape[1]
    exp_lanes = -(-experts // 128) * 128
    s.static_out[...] = jnp.zeros_like(s.static_out)

    def padded(value):
        return jnp.concatenate([value.astype(F32), jnp.zeros((pitch - columns, value.shape[1]), F32)], axis=0).astype(BF16)

    s.static_out[:, pl.ds(0, tokens)] = padded(s.residual[...])
    s.static_out[:, pl.ds(tok_lanes, experts)] = padded(s.centroid[...])
    gain_row = jnp.broadcast_to(s.gain[...].astype(F32), (pitch, columns))
    diagonal = iota((pitch, columns), 0) == iota((pitch, columns), 1)
    gain_col = jnp.sum(jnp.where(diagonal, gain_row, 0.0), axis=1, keepdims=True)
    first_lane = iota((pitch, 128), 1) == 0
    s.static_out[:, pl.ds(tok_lanes + exp_lanes, 128)] = jnp.where(first_lane, gain_col, 0.0).astype(BF16)

    own_rows = pl.ds(pl.multiple_of(owner * pitch, pitch), pitch)
    cols_copies = []
    static_copies = []
    for dh in range(1, heads):
        to_head = (head + dh) % heads
        lanes = pl.ds(pl.multiple_of(to_head * head_features, 128), head_features)
        cols_copies.append(push(s.cols_out.at[:, lanes], s.cols_in.at[own_rows], s.cols_sem, dh - 1, rep, to_head))
        static_copies.append(push(s.static_out, s.static_in.at[own_rows], s.static_sem, dh - 1, rep, to_head))
    own_lanes = pl.ds(pl.multiple_of(head * head_features, 128), head_features)
    own_cols = pltpu.make_async_copy(s.cols_out.at[:, own_lanes], s.cols_in.at[own_rows], s.load_sem.at[13])
    own_cols.start()
    own_static = pltpu.make_async_copy(s.static_out, s.static_in.at[own_rows], s.load_sem.at[14])
    own_static.start()

    load_cache.wait()
    for i in range(RES):
        scores = nn(joined_query(i), s.cache[i]) * scale
        weights = jnp.exp(scores - jnp.max(scores, axis=1, keepdims=True))
        weights = (weights / jnp.sum(weights, axis=1, keepdims=True)).astype(BF16)
        keep_latents(i, nt(weights, s.cache[i, pl.ds(0, kv), :]))

    def head_outputs(start, count):
        for h in range(16):
            at = pl.ds(16 * start + h, count, stride=16) if count > 1 else pl.ds(16 * start + h, 1)
            parts = [s.latents[i, at, :] for i in range(kv // 128)]
            part = jnp.concatenate(parts, axis=1).astype(BF16)
            s.heads_f[at, :] = nn(part, s.value[h])
        return s.heads_f[pl.ds(16 * start, 16 * count), :].astype(BF16)

    load_value.wait()
    s.near_out[...] = head_outputs(0, RES)
    near_copies = []
    for k, (dx, dz) in enumerate(line_offsets):
        near_copies.append(push(s.near_out, s.near_in.at[line], s.near_sem, k, rep_at(dx, dz, 0), head))
    s.near_in[line] = s.near_out[...]
    load_up = load(up_hbm, s.up, 15)
    chunk = zs * line_columns
    load_down = [load(down_hbm.at[:, pl.ds(i * chunk, chunk)], s.down.at[i], 16 + i) for i in range(xs)]

    for copy in cols_copies + static_copies:
        copy.wait_recv()
    own_cols.wait()
    own_static.wait()
    core_rows = pl.ds(pl.multiple_of(core * (heads * pitch), heads * pitch), heads * pitch)
    other = rep_at(0, 0, 1)
    cols_pass = push(s.cols_in.at[core_rows], s.cols_in.at[core_rows], s.cols_sem, heads - 1, other, head)
    static_pass = push(s.static_in.at[core_rows], s.static_in.at[core_rows], s.static_sem, heads - 1, other, head)

    held = iota((tokens, tokens), 0)
    resident = held < CORES * near
    held_in = jnp.where(resident, held, held - CORES * near)
    held_size = jnp.where(resident, near, lines)
    held_core = jnp.where(held_in >= held_size, 1, 0)
    held_in = held_in - held_size * held_core
    held_line = jnp.where(resident, held_in >> 3, held_in)
    held_row = jnp.where(resident, held_in & (RES - 1), RES)
    order = batch * (CORES * held_line + held_core) + held_row
    reorder = one_hot(iota((tokens, tokens), 1) == order)
    s.reorder[...] = reorder
    named = jnp.zeros((lines, tokens), F32)
    my_experts = iota((lines, tokens), 0) * (CORES * heads) + owner
    for k in range(ids_hbm.shape[0]):
        named = jnp.where(my_experts == s.ids[pl.ds(k, 1), :], 1.0, named)
    earlier = one_hot(iota((tokens, tokens), 0) < iota((tokens, tokens), 1))
    slot = jnp.where(named > 0.0, nn(named.astype(BF16), earlier), -1.0)
    slot_index = iota((SLOTS, tokens), 0).astype(F32)
    pieces = [jnp.where(slot[e:e + 1, :] == slot_index, 1.0, 0.0) for e in range(lines)]
    s.gather[...] = jnp.concatenate(pieces, axis=0).astype(BF16)
    s.gather_held[...] = nt(s.gather[...], reorder).astype(BF16)
    eye = one_hot(iota((tokens, tokens), 0) == iota((tokens, tokens), 1))
    s.scatter[...] = nt(eye, s.gather[...]).astype(BF16)

    row_count = reps * moved_n
    pair = CORES * moved_n

    def keep_rows(from_line):
        both = [s.moved_in[from_line * CORES + c].astype(F32) for c in range(CORES)]
        s.rows_b[pl.ds(pl.multiple_of(from_line * pair, pair), pair), :] = jnp.concatenate(both, axis=0).astype(BF16)

    s.moved_in[rep] = s.moved_out[rep]
    rows_copies[-1].wait_recv()
    keep_rows(line)
    for i, (dx, dz) in enumerate(line_offsets):
        for copy in rows_copies[CORES * i:CORES * i + CORES]:
            copy.wait_recv()
        keep_rows(line_at(-dx, -dz))
    for copy in query_copies:
        copy.wait_recv()
    far_all = jnp.concatenate([s.far_queries[h] for h in range(heads)], axis=0)
    far_scores = nt(far_all, s.rows_b[...]) * scale
    place = iota((1, row_count), 1)
    from_device = (place * 2731) >> 16
    position = place + from_device * (moved_n * (heads - 1)) + head * moved_n
    far_scores = jnp.where(position < length, far_scores, -1e30)
    far_max = jnp.max(far_scores, axis=1, keepdims=True)
    far_weights = jnp.exp(far_scores - far_max)
    far_sum = jnp.sum(far_weights, axis=1, keepdims=True)
    s.far_out[:, pl.ds(0, kv)] = nn(far_weights.astype(BF16), s.rows_b[:, pl.ds(0, kv)]).astype(BF16)
    lane = iota((heads * 16, 128), 1)
    max_high = far_max.astype(BF16).astype(F32)
    max_mid = (far_max - max_high).astype(BF16).astype(F32)
    max_low = far_max - max_high - max_mid
    sum_high, sum_low = split2(far_sum)
    extras = jnp.zeros((heads * 16, 128), F32)
    for i, extra in enumerate((max_high, max_mid, max_low, sum_high, sum_low)):
        extras = jnp.where(lane == i, extra, extras)
    s.far_out[:, pl.ds(kv, 128)] = extras.astype(BF16)
    far_copies = []
    for dh in range(1, heads):
        to_head = (head + dh) % heads
        their_rows = pl.ds(pl.multiple_of(to_head * 16, 16), 16)
        far_copies.append(push(s.far_out.at[their_rows], s.far_in.at[head], s.far_sem, dh - 1, rep, to_head))
    s.far_in[head] = s.far_out[pl.ds(pl.multiple_of(head * 16, 16), 16), :]
    cols_pass.wait_recv()
    static_pass.wait_recv()
    row = iota((width, width), 0)
    col = iota((width, width), 1)
    squeeze = one_hot((row < line_columns) & (col == row + (pitch - columns) * ((row * 2341) >> 16)))
    for i in range(head_features // 512):
        cut = pl.ds(512 * i, 512)
        s.cols[:, cut] = nn(squeeze, s.cols_in[:, cut]).astype(BF16)
    static = nn(squeeze, s.static_in[...]).astype(BF16)
    s.residual_c[...] = nt(reorder, static[:, :tokens])
    their_expert = iota((lines, experts), 0) * (CORES * heads) + owner
    pick = one_hot(iota((lines, experts), 1) == their_expert)
    s.centroid_c[...] = nt(pick, static[:, tok_lanes:tok_lanes + experts])
    first = one_hot((iota((8, 128), 0) == 0) & (iota((8, 128), 1) == 0))
    s.gain_c[...] = nt(first, static[:, tok_lanes + exp_lanes:])
    for copy in far_copies:
        copy.wait_recv()
    extras = [s.far_in[h, :, pl.ds(kv, 128)].astype(F32) for h in range(heads)]
    maxima = [extra[:, 0:1] + extra[:, 1:2] + extra[:, 2:3] for extra in extras]
    top = functools.reduce(jnp.maximum, maxima)
    total = jnp.zeros((16, kv), F32)
    weight_sum = jnp.zeros((16, 1), F32)
    for h in range(heads):
        factor = jnp.exp(maxima[h] - top)
        total = total + factor * s.far_in[h, :, pl.ds(0, kv)].astype(F32)
        weight_sum = weight_sum + factor * (extras[h][:, 3:4] + extras[h][:, 4:5])
    keep_latents(RES, total / weight_sum)
    s.far_heads_out[...] = head_outputs(RES, 1)
    far_head_copies = []
    for k, (dx, dz) in enumerate(line_offsets):
        far_head_copies.append(push(s.far_heads_out, s.far_heads_in.at[line], s.heads_sem, k, rep_at(dx, dz, 0), head))
    s.far_heads_in[line] = s.far_heads_out[...]


    def project(copies, arrived, wide, count):
        for copy in copies:
            copy.wait_recv()
        wide[...] = arrived[...].astype(F32).reshape(wide.shape)
        acts = [wide[pl.ds(h, count, stride=16), :].astype(BF16) for h in range(16)]
        return nt(jnp.concatenate(acts, axis=1), s.cols[...])

    def spread_sum(part):
        s.sum_out[...] = part.astype(BF16)
        return [
            push(s.sum_out, s.sum_in.at[dh - 1], s.near_sum_sem, dh - 1, rep, (head + dh) % heads)
            for dh in range(1, heads)
        ]

    def swap_sum(part, copies):
        for dh, copy in enumerate(copies):
            copy.wait_recv()
            part = part + s.sum_in[dh].astype(F32)
        s.swap_out[...] = part
        return push(s.swap_out, s.swap_in, s.swap_sem, 0, other, head)

    near_part = project(near_copies, s.near_in, s.near_w, near)
    near_sums = spread_sum(near_part)
    far_part = project(far_head_copies, s.far_heads_in, s.far_w, lines)
    s.far_sum_out[...] = far_part.astype(BF16)
    far_sums = []
    for k, (dc, dh) in enumerate(line_places):
        far_sums.append(push(s.far_sum_out, s.far_sum_in.at[k], s.sum_sem, k, rep_at(0, 0, dc), (head + dh) % heads))
    near_swap = swap_sum(near_part, near_sums)
    first_core = core == 0
    near_tokens = CORES * near
    near_swap.wait_recv()

    def by_core(mine, theirs):
        return jnp.concatenate([jnp.where(first_core, mine, theirs), jnp.where(first_core, theirs, mine)], axis=0)

    def scaled_rows(attended, start, count):
        here = pl.ds(start, count)
        combined = s.residual_c[here, :] + attended
        s.combined[here, :] = combined
        square_high, square_low = split2(jnp.sum(combined * combined, axis=1, keepdims=True))
        scaled = combined * s.gain_c[0:1, :]
        token_lane = iota((count, width), 1)
        scaled = jnp.where(token_lane == line_columns, square_high, scaled)
        return jnp.where(token_lane == line_columns + 1, square_low, scaled).astype(BF16)

    near_scaled = scaled_rows(by_core(s.swap_out[...], s.swap_in[...]), 0, near_tokens)
    gathered = nn(s.gather_held[:, pl.ds(0, near_tokens)], near_scaled)
    far_mine = far_part
    far_theirs = jnp.zeros_like(far_part)
    for k, (dc, dh) in enumerate(line_places):
        far_sums[k].wait_recv()
        if dc == 0:
            far_mine = far_mine + s.far_sum_in[k].astype(F32)
        else:
            far_theirs = far_theirs + s.far_sum_in[k].astype(F32)
    far_scaled = scaled_rows(by_core(far_mine, far_theirs), near_tokens, CORES * lines)
    gathered = gathered + nn(s.gather_held[:, pl.ds(near_tokens, CORES * lines)], far_scaled)
    slot_lane = iota((SLOTS, width), 1)
    for e in range(lines):
        rows = gathered[SLOTS * e:SLOTS * e + SLOTS]
        high, low = split2(jnp.sum(rows * s.centroid_c[e:e + 1, :], axis=1, keepdims=True))
        rows = jnp.where(slot_lane == line_columns + 2, high, rows)
        rows = jnp.where(slot_lane == line_columns + 3, low, rows)
        s.tok_out[e] = rows.astype(BF16)
    tok_copies = []
    for k, (dx, dz) in enumerate(line_offsets):
        tok_copies.append(push(s.tok_out.at[line_at(dx, dz)], s.tok_in.at[line], s.tok_sem, k, rep_at(dx, dz, 0), head))
    s.tok_in[line] = s.tok_out[line]

    load_up.wait()
    inner = nn(s.tok_in[line][:, :line_columns], s.up[line])
    stats = s.tok_in[line].astype(F32)[:, width - 128:]
    for copy, (dx, dz) in zip(tok_copies, line_offsets):
        copy.wait_recv()
        from_line = line_at(-dx, -dz)
        rows = s.tok_in[from_line]
        inner = inner + nn(rows[:, :line_columns], s.up[from_line])
        stats = stats + rows.astype(F32)[:, width - 128:]
    at = line_columns - (width - 128)
    squares = stats[:, at:at + 1] + stats[:, at + 1:at + 2]
    logit = stats[:, at + 2:at + 3] + stats[:, at + 3:at + 4]
    root_mean = jnp.sqrt(squares / features + 1e-6)
    inner = inner / root_mean
    hidden = (inner * jax.nn.sigmoid(inner)).astype(BF16)
    affinity = jax.nn.sigmoid(logit / root_mean)
    affinity_high, affinity_low = split2(affinity)
    for copy in load_down:
        copy.wait()
    back_copies = []
    filler = jnp.zeros((SLOTS, width - line_columns), F32)
    x_order = sorted(range(xs), key=lambda dx: -min(dx, xs - dx))
    for dx in x_order:
        to_x = (lx + dx) % xs
        result = nn(hidden, s.down[to_x]) * affinity
        for z in range(zs):
            piece = jnp.concatenate([result[:, z * line_columns:(z + 1) * line_columns], filler], axis=1)
            piece = jnp.where(slot_lane == line_columns, affinity_high, piece)
            piece = jnp.where(slot_lane == line_columns + 1, affinity_low, piece)
            s.back_out[to_x * zs + z] = piece.astype(BF16)
        for dz in range(zs):
            if (dx, dz) != (0, 0):
                k = line_offsets.index((dx, dz))
                back_copies.append((k, push(s.back_out.at[line_at(dx, dz)], s.back_in.at[line], s.back_sem, k, rep_at(dx, dz, 0), head)))
    s.back_in[line] = s.back_out[line]
    rest = s.combined[...]
    my_columns = one_hot((iota((pitch, width), 0) < columns) & (iota((pitch, width), 1) == owner * columns + iota((pitch, width), 0)))
    combined_own = jnp.zeros((pitch, tokens), F32)
    for _ in range(3):
        part = rest.astype(BF16)
        rest = rest - part.astype(F32)
        combined_own = combined_own + nn(nt(my_columns, part).astype(BF16), s.reorder[...])
    s.combined_own[...] = combined_own

    for _, copy in back_copies:
        copy.wait_recv()

    returned = jnp.concatenate([s.back_in[e].astype(F32) for e in range(lines)], axis=0).astype(BF16)
    summed = nn(s.scatter[...], returned)
    token_lane = iota((tokens, width), 1)
    share_high, share_low = split2(summed[:, line_columns:line_columns + 1] + summed[:, line_columns + 1:line_columns + 2])
    summed = jnp.where(token_lane == line_columns, share_high, summed)
    summed = jnp.where(token_lane == line_columns + 1, share_low, summed)
    place_in = row & (pitch - 1)
    wanted = jnp.where(place_in < columns, row - (pitch - columns) * (row // pitch), line_columns + place_in - columns)
    spread = one_hot((col == wanted) & (place_in < columns + 2))
    pieces = nt(spread, summed.astype(BF16)).astype(BF16)
    for j in range(CORES * heads):
        s.last_out[j] = pieces[pitch * j:pitch * j + pitch]
    last_copies = []
    for k, (dc, dh) in enumerate(line_places):
        to_core, to_head = (core + dc) % CORES, (head + dh) % heads
        last_copies.append(push(
            s.last_out.at[to_core * heads + to_head], s.last_in.at[owner], s.last_sem, k, rep_at(0, 0, dc), to_head))
    s.last_in[owner] = s.last_out[owner]
    for copy in last_copies:
        copy.wait_recv()
    routed = s.last_in[0].astype(F32)
    for j in range(1, CORES * heads):
        routed = routed + s.last_in[j].astype(F32)
    share = routed[columns:columns + 1] + routed[columns + 1:columns + 2]
    layer_out = s.combined_own[...] + 2.5 * routed / share
    out_ref[...] = layer_out[:columns].astype(BF16)

    sends = rows_copies + cols_copies + static_copies + [cols_pass, static_pass] + query_copies + far_copies
    sends += near_copies + far_head_copies + near_sums + far_sums + [near_swap] + tok_copies + [copy for _, copy in back_copies] + last_copies
    for copy in sends:
        copy.wait_send()


def per_device(
    query, latent_cache, moved_rows, target_group, moved_length, key_absorb, value_head_projection,
    out_proj, residual, norm_gain, centroid, expert_ids, up_weight, down_weight,
):
    reps = lax.axis_size("rep")
    heads = lax.axis_size("head")
    lines = reps // CORES
    xs = 4 if lines % 4 == 0 else lines
    zs = lines // xs
    groups, moved_n, full = moved_rows.shape
    batch, local_heads, qdim = query.shape
    columns = out_proj.shape[1]
    tokens, topk = expert_ids.shape
    features, hidden = up_weight.shape[1:]
    experts = centroid.shape[0]
    kv = value_head_projection.shape[1]
    vd = value_head_projection.shape[2]
    context = latent_cache.shape[1]
    line_columns = columns * CORES * heads
    width = -(-line_columns // 128) * 128
    pitch = -(-columns // 16) * 16
    half = tokens // CORES
    tok_lanes = -(-tokens // 128) * 128
    static_lanes = tok_lanes + -(-experts // 128) * 128 + 128
    head_features = local_heads * vd

    vmem = dict(
        target=((1, groups), jnp.int32),
        length=((1, groups), jnp.int32),
        source_v=((groups, 128), jnp.int32),
        moved=((groups, moved_n, full), BF16),
        moved_out=((groups, moved_n, full), BF16),
        moved_in=((reps, moved_n, full), BF16),
        rows_b=((reps * moved_n, full), BF16),
        query=((batch * local_heads, qdim), BF16),
        query_f=((batch * local_heads, 128), F32),
        absorb=(key_absorb.shape, BF16),
        value=(value_head_projection.shape, BF16),
        cache=((latent_cache.shape[0], full, context), BF16),
        outproj=((columns, out_proj.shape[0]), BF16),
        cols_out=((pitch, out_proj.shape[0]), BF16),
        cols_in=((pitch * CORES * heads, head_features), BF16),
        cols=((width, head_features), BF16),
        residual=((columns, tokens), BF16),
        gain=((1, columns), BF16),
        centroid=((columns, experts), BF16),
        ids=((topk, tokens), jnp.int32),
        static_out=((pitch, static_lanes), BF16),
        static_in=((pitch * CORES * heads, static_lanes), BF16),
        residual_c=((tokens, width), F32),
        centroid_c=((lines, width), F32),
        gain_c=((8, width), F32),
        reorder=((tokens, tokens), BF16),
        gather=((lines * SLOTS, tokens), BF16),
        gather_held=((lines * SLOTS, tokens), BF16),
        scatter=((tokens, lines * SLOTS), BF16),
        joined=((kv // 128 + 1, batch * local_heads, 128), F32),
        latents=((kv // 128, batch * local_heads, 128), F32),
        heads_f=((batch * local_heads, vd), F32),
        near_out=((RES * local_heads, vd), BF16),
        near_in=((lines, RES * local_heads, vd), BF16),
        near_w=((lines * RES * local_heads, vd), F32),
        far_heads_out=((local_heads, vd), BF16),
        far_heads_in=((lines, local_heads, vd), BF16),
        far_w=((lines * local_heads, vd), F32),
        far_query=((local_heads, full), BF16),
        far_queries=((heads, local_heads, full), BF16),
        far_out=((heads * local_heads, kv + 128), BF16),
        far_in=((heads, local_heads, kv + 128), BF16),
        sum_out=((lines * RES, width), BF16),
        sum_in=((heads - 1, lines * RES, width), BF16),
        far_sum_out=((lines, width), BF16),
        far_sum_in=((CORES * heads - 1, lines, width), BF16),
        swap_out=((lines * RES, width), F32),
        swap_in=((lines * RES, width), F32),
        combined=((tokens, width), F32),
        combined_own=((pitch, tokens), F32),
        tok_out=((lines, SLOTS, width), BF16),
        tok_in=((lines, SLOTS, width), BF16),
        up=((lines, line_columns, hidden), BF16),
        down=((xs, hidden, zs * line_columns), BF16),
        back_out=((lines, SLOTS, width), BF16),
        back_in=((lines, SLOTS, width), BF16),
        last_out=((CORES * heads, pitch, tokens), BF16),
        last_in=((CORES * heads, pitch, tokens), BF16),
    )
    sems = dict(
        load_sem=(16 + xs,), rows_sem=(2, reps - 1), cols_sem=(2, heads), static_sem=(2, heads),
        query_sem=(2, heads - 1), far_sem=(2, heads - 1), heads_sem=(2, lines - 1), sum_sem=(2, CORES * heads - 1),
        swap_sem=(2, 1), near_sem=(2, lines - 1), near_sum_sem=(2, heads - 1), tok_sem=(2, lines - 1), back_sem=(2, lines - 1), last_sem=(2, CORES * heads - 1),
    )
    names = list(vmem) + ["source_s"] + list(sems)
    scratch = [pltpu.VMEM(shape, dtype) for shape, dtype in vmem.values()]
    scratch += [pltpu.SMEM((groups, 128), jnp.int32)]
    scratch += [pltpu.SemaphoreType.DMA(shape) for shape in sems.values()]
    dims = (reps, heads, lines, xs, zs, groups, moved_n, columns, tokens, features)
    layer_out = pl.pallas_call(
        functools.partial(layer_kernel, names, dims),
        out_shape=jax.ShapeDtypeStruct((columns, tokens), BF16),
        in_specs=[pl.BlockSpec(memory_space=pl.ANY)] * 14,
        out_specs=pl.BlockSpec(memory_space=pltpu.VMEM),
        scratch_shapes=scratch,
        compiler_params=pltpu.CompilerParams(
            collective_id=0, has_side_effects=True, vmem_limit_bytes=60 * 1024 * 1024
        ),
        name="latent_moe_layer",
    )(
        target_group.reshape(1, groups), moved_length.reshape(1, groups), query.reshape(batch * local_heads, qdim), jnp.swapaxes(latent_cache, 1, 2), moved_rows,
        key_absorb, value_head_projection, out_proj.T, residual.T, norm_gain.reshape(1, columns), centroid.T,
        expert_ids.T, up_weight.reshape(lines, line_columns, hidden), down_weight[0],
    )
    return layer_out.T


def solution(mesh):
    return jax.shard_map(
        per_device,
        mesh=mesh,
        in_specs=(
            P("rep", "head", None),
            P("rep", None, None),
            P(None, ("rep", "head"), None),
            P(),
            P(),
            P("head", None, None),
            P("head", None, None),
            P(None, ("rep", "head")),
            P(None, ("rep", "head")),
            P(("rep", "head")),
            P(None, ("rep", "head")),
            P(),
            P(("rep", "head"), None, None),
            P(("rep", "head"), None, None),
        ),
        out_specs=P(None, ("rep", "head")),
        check_vma=False,
    )
```

```python
import functools
import math
import types

import jax
import jax.numpy as jnp
from jax import lax
from jax.experimental import pallas as pl
from jax.experimental.pallas import tpu as pltpu
from jax.sharding import PartitionSpec as P

MESH = pl.DeviceIdType.MESH
F32 = jnp.float32
BF16 = jnp.bfloat16
RES = 8
SLOTS = 40
CORES = 2


def nn(a, b):
    return lax.dot_general(a, b, (((1,), (0,)), ((), ())), preferred_element_type=F32)


def nt(a, b):
    return lax.dot_general(a, b, (((1,), (1,)), ((), ())), preferred_element_type=F32)


def one_hot(mask):
    return jnp.where(mask, 1.0, 0.0).astype(BF16)


def iota(shape, dim):
    return lax.broadcasted_iota(jnp.int32, shape, dim)


def split2(value):
    high = value.astype(BF16).astype(F32)
    return high, (value - high).astype(BF16).astype(F32)


def layer_kernel(names, dims, *refs):
    (
        target_hbm, length_hbm, query_hbm, cache_hbm, moved_hbm, absorb_hbm, value_hbm, outproj_hbm,
        residual_hbm, gain_hbm, centroid_hbm, ids_hbm, up_hbm, down_hbm, out_ref,
    ) = refs[:15]
    s = types.SimpleNamespace(**dict(zip(names, refs[15:])))
    reps, heads, lines, xs, zs, groups, moved_n, columns, tokens, features = dims
    line_columns = columns * CORES * heads
    width = -(-line_columns // 128) * 128
    pitch = -(-columns // 16) * 16
    batch = tokens // reps
    half = lines * batch
    near = lines * RES
    kv = value_hbm.shape[1]
    nope = absorb_hbm.shape[1]
    qdim = query_hbm.shape[1]
    rope = qdim - nope
    full = kv + rope
    head_features = 16 * value_hbm.shape[2]
    scale = 1.0 / math.sqrt(qdim)

    rep = lax.axis_index("rep")
    head = lax.axis_index("head")
    line = rep // CORES
    core = rep % CORES
    lx = line // zs
    lz = line % zs
    owner = core * heads + head

    next_x = [(lx + d) % xs for d in range(xs)]
    next_z = [(lz + d) % zs for d in range(zs)]
    next_core = [(core + d) % CORES for d in range(CORES)]

    def line_at(dx, dz):
        return next_x[dx % xs] * zs + next_z[dz % zs]

    def rep_at(dx, dz, dc):
        return line_at(dx, dz) * CORES + next_core[dc % CORES]

    line_offsets = [(dx, dz) for dx in range(xs) for dz in range(zs) if (dx, dz) != (0, 0)]
    line_offsets.sort(key=lambda o: -(min(o[0], xs - o[0]) + min(o[1], zs - o[1])))
    plane_offsets = [(dx, dz, dc) for dx, dz in line_offsets for dc in range(CORES)]
    plane_offsets += [(0, 0, dc) for dc in range(1, CORES)]

    line_places = [(dc, dh) for dc in range(CORES) for dh in range(heads) if (dc, dh) != (0, 0)]

    def load(src, dst, sem):
        copy = pltpu.make_async_copy(src, dst, s.load_sem.at[sem])
        copy.start()
        return copy

    load_target = load(target_hbm, s.target, 0)
    load_length = load(length_hbm, s.length, 1)
    load_moved = load(moved_hbm, s.moved, 2)

    barrier = pltpu.get_barrier_semaphore()
    partners = [(rep_at(*o), head) for o in plane_offsets]
    for dh in range(1, heads):
        for dc in range(CORES):
            partners.append((rep_at(0, 0, dc), (head + dh) % heads))
    for partner in partners[:12]:
        pl.semaphore_signal(barrier, inc=1, device_id=partner, device_id_type=MESH)
    load_target.wait()
    load_length.wait()
    matches = iota((groups, groups), 0) == s.target[...]
    source = jnp.sum(jnp.where(matches, iota((groups, groups), 1), 0), axis=1, keepdims=True)
    s.source_v[...] = jnp.broadcast_to(source, (groups, 128))
    load_source = load(s.source_v, s.source_s, 12)
    my_match = matches & (iota((groups, groups), 0) == rep)
    length = jnp.sum(jnp.sum(jnp.where(my_match, s.length[...], 0), axis=1, keepdims=True), axis=0, keepdims=True)
    for partner in partners[12:]:
        pl.semaphore_signal(barrier, inc=1, device_id=partner, device_id_type=MESH)
    load_query = load(query_hbm, s.query, 3)
    load_absorb = load(absorb_hbm, s.absorb, 4)
    load_cache = load(cache_hbm, s.cache, 5)
    load_ids = load(ids_hbm, s.ids, 6)
    load_residual = load(residual_hbm, s.residual, 7)
    load_gain = load(gain_hbm, s.gain, 8)
    load_centroid = load(centroid_hbm, s.centroid, 9)
    load_outproj = load(outproj_hbm, s.outproj, 10)
    load_value = load(value_hbm, s.value, 11)

    load_source.wait()
    load_moved.wait()
    for g in range(groups):
        s.moved_out[g] = s.moved[jnp.clip(s.source_s[g, 0], 0, groups - 1)]


    pl.semaphore_wait(barrier, len(partners))

    def push(src, dst, phase, k, to_rep, to_head):
        copy = pltpu.make_async_remote_copy(
            src_ref=src, dst_ref=dst, send_sem=phase.at[0, k], recv_sem=phase.at[1, k],
            device_id=(to_rep, to_head), device_id_type=MESH,
        )
        copy.start()
        return copy

    rows_copies = []
    for k, offset in enumerate(plane_offsets):
        to_rep = rep_at(*offset)
        rows_copies.append(push(s.moved_out.at[to_rep], s.moved_in.at[rep], s.rows_sem, k, to_rep, head))

    load_query.wait()
    s.query_f[...] = s.query[:, pl.ds(0, nope)].astype(F32)
    s.joined[kv // 128, :, pl.ds(0, rope)] = s.query[:, pl.ds(nope, rope)].astype(F32)
    load_absorb.wait()
    for h in range(16):
        part = s.query_f[pl.ds(h, batch, stride=16), :].astype(BF16)
        absorbed = nn(part, s.absorb[h])
        for i in range(kv // 128):
            s.joined[i, pl.ds(h, batch, stride=16), :] = absorbed[:, 128 * i:128 * i + 128]

    def joined_query(i):
        parts = [s.joined[j, pl.ds(16 * i, 16), :] for j in range(kv // 128)]
        parts.append(s.joined[kv // 128, pl.ds(16 * i, 16), pl.ds(0, rope)])
        return jnp.concatenate(parts, axis=1).astype(BF16)

    def keep_latents(i, value):
        for j in range(kv // 128):
            s.latents[j, pl.ds(16 * i, 16), :] = value[:, 128 * j:128 * j + 128]

    s.far_query[...] = joined_query(RES)
    query_copies = []
    for dh in range(1, heads):
        query_copies.append(push(s.far_query, s.far_queries.at[head], s.query_sem, dh - 1, rep, (head + dh) % heads))
    s.far_queries[head] = s.far_query[...]

    load_outproj.wait()
    pad = jnp.zeros((pitch - columns, 512), F32)
    for i in range(outproj_hbm.shape[1] // 512):
        cut = s.outproj[:, pl.ds(512 * i, 512)].astype(F32)
        s.cols_out[:, pl.ds(512 * i, 512)] = jnp.concatenate([cut, pad], axis=0).astype(BF16)
    for copy in (load_residual, load_gain, load_centroid, load_ids):
        copy.wait()
    tok_lanes = -(-tokens // 128) * 128
    experts = centroid_hbm.shape[1]
    exp_lanes = -(-experts // 128) * 128
    s.static_out[...] = jnp.zeros_like(s.static_out)

    def padded(value):
        return jnp.concatenate([value.astype(F32), jnp.zeros((pitch - columns, value.shape[1]), F32)], axis=0).astype(BF16)

    s.static_out[:, pl.ds(0, tokens)] = padded(s.residual[...])
    s.static_out[:, pl.ds(tok_lanes, experts)] = padded(s.centroid[...])
    gain_row = jnp.broadcast_to(s.gain[...].astype(F32), (pitch, columns))
    diagonal = iota((pitch, columns), 0) == iota((pitch, columns), 1)
    gain_col = jnp.sum(jnp.where(diagonal, gain_row, 0.0), axis=1, keepdims=True)
    first_lane = iota((pitch, 128), 1) == 0
    s.static_out[:, pl.ds(tok_lanes + exp_lanes, 128)] = jnp.where(first_lane, gain_col, 0.0).astype(BF16)

    own_rows = pl.ds(pl.multiple_of(owner * pitch, pitch), pitch)
    cols_copies = []
    static_copies = []
    for dh in range(1, heads):
        to_head = (head + dh) % heads
        lanes = pl.ds(pl.multiple_of(to_head * head_features, 128), head_features)
        cols_copies.append(push(s.cols_out.at[:, lanes], s.cols_in.at[own_rows], s.cols_sem, dh - 1, rep, to_head))
        static_copies.append(push(s.static_out, s.static_in.at[own_rows], s.static_sem, dh - 1, rep, to_head))
    own_lanes = pl.ds(pl.multiple_of(head * head_features, 128), head_features)
    own_cols = pltpu.make_async_copy(s.cols_out.at[:, own_lanes], s.cols_in.at[own_rows], s.load_sem.at[13])
    own_cols.start()
    own_static = pltpu.make_async_copy(s.static_out, s.static_in.at[own_rows], s.load_sem.at[14])
    own_static.start()

    load_cache.wait()
    for i in range(RES):
        scores = nn(joined_query(i), s.cache[i]) * scale
        weights = jnp.exp(scores - jnp.max(scores, axis=1, keepdims=True))
        weights = (weights / jnp.sum(weights, axis=1, keepdims=True)).astype(BF16)
        keep_latents(i, nt(weights, s.cache[i, pl.ds(0, kv), :]))

    def head_outputs(start, count):
        for h in range(16):
            at = pl.ds(16 * start + h, count, stride=16) if count > 1 else pl.ds(16 * start + h, 1)
            parts = [s.latents[i, at, :] for i in range(kv // 128)]
            part = jnp.concatenate(parts, axis=1).astype(BF16)
            s.heads_f[at, :] = nn(part, s.value[h])
        return s.heads_f[pl.ds(16 * start, 16 * count), :].astype(BF16)

    load_value.wait()
    s.near_out[...] = head_outputs(0, RES)
    near_copies = []
    for k, (dx, dz) in enumerate(line_offsets):
        near_copies.append(push(s.near_out, s.near_in.at[line], s.near_sem, k, rep_at(dx, dz, 0), head))
    s.near_in[line] = s.near_out[...]
    load_up = load(up_hbm, s.up, 15)
    chunk = zs * line_columns
    load_down = [load(down_hbm.at[:, pl.ds(i * chunk, chunk)], s.down.at[i], 16 + i) for i in range(xs)]

    for copy in cols_copies + static_copies:
        copy.wait_recv()
    own_cols.wait()
    own_static.wait()
    core_rows = pl.ds(pl.multiple_of(core * (heads * pitch), heads * pitch), heads * pitch)
    other = rep_at(0, 0, 1)
    cols_pass = push(s.cols_in.at[core_rows], s.cols_in.at[core_rows], s.cols_sem, heads - 1, other, head)
    static_pass = push(s.static_in.at[core_rows], s.static_in.at[core_rows], s.static_sem, heads - 1, other, head)

    held = iota((tokens, tokens), 0)
    resident = held < CORES * near
    held_in = jnp.where(resident, held, held - CORES * near)
    held_size = jnp.where(resident, near, lines)
    held_core = jnp.where(held_in >= held_size, 1, 0)
    held_in = held_in - held_size * held_core
    held_line = jnp.where(resident, held_in >> 3, held_in)
    held_row = jnp.where(resident, held_in & (RES - 1), RES)
    order = batch * (CORES * held_line + held_core) + held_row
    reorder = one_hot(iota((tokens, tokens), 1) == order)
    s.reorder[...] = reorder
    named = jnp.zeros((lines, tokens), F32)
    my_experts = iota((lines, tokens), 0) * (CORES * heads) + owner
    for k in range(ids_hbm.shape[0]):
        named = jnp.where(my_experts == s.ids[pl.ds(k, 1), :], 1.0, named)
    earlier = one_hot(iota((tokens, tokens), 0) < iota((tokens, tokens), 1))
    slot = jnp.where(named > 0.0, nn(named.astype(BF16), earlier), -1.0)
    slot_index = iota((SLOTS, tokens), 0).astype(F32)
    pieces = [jnp.where(slot[e:e + 1, :] == slot_index, 1.0, 0.0) for e in range(lines)]
    s.gather[...] = jnp.concatenate(pieces, axis=0).astype(BF16)
    s.gather_held[...] = nt(s.gather[...], reorder).astype(BF16)
    eye = one_hot(iota((tokens, tokens), 0) == iota((tokens, tokens), 1))
    s.scatter[...] = nt(eye, s.gather[...]).astype(BF16)

    row_count = reps * moved_n
    pair = CORES * moved_n

    def keep_rows(from_line):
        both = [s.moved_in[from_line * CORES + c].astype(F32) for c in range(CORES)]
        s.rows_b[pl.ds(pl.multiple_of(from_line * pair, pair), pair), :] = jnp.concatenate(both, axis=0).astype(BF16)

    s.moved_in[rep] = s.moved_out[rep]
    rows_copies[-1].wait_recv()
    keep_rows(line)
    for i, (dx, dz) in enumerate(line_offsets):
        for copy in rows_copies[CORES * i:CORES * i + CORES]:
            copy.wait_recv()
        keep_rows(line_at(-dx, -dz))
    for copy in query_copies:
        copy.wait_recv()
    far_all = jnp.concatenate([s.far_queries[h] for h in range(heads)], axis=0)
    far_scores = nt(far_all, s.rows_b[...]) * scale
    place = iota((1, row_count), 1)
    from_device = (place * 2731) >> 16
    position = place + from_device * (moved_n * (heads - 1)) + head * moved_n
    far_scores = jnp.where(position < length, far_scores, -1e30)
    far_max = jnp.max(far_scores, axis=1, keepdims=True)
    far_weights = jnp.exp(far_scores - far_max)
    far_sum = jnp.sum(far_weights, axis=1, keepdims=True)
    s.far_out[:, pl.ds(0, kv)] = nn(far_weights.astype(BF16), s.rows_b[:, pl.ds(0, kv)]).astype(BF16)
    lane = iota((heads * 16, 128), 1)
    max_high = far_max.astype(BF16).astype(F32)
    max_mid = (far_max - max_high).astype(BF16).astype(F32)
    max_low = far_max - max_high - max_mid
    sum_high, sum_low = split2(far_sum)
    extras = jnp.zeros((heads * 16, 128), F32)
    for i, extra in enumerate((max_high, max_mid, max_low, sum_high, sum_low)):
        extras = jnp.where(lane == i, extra, extras)
    s.far_out[:, pl.ds(kv, 128)] = extras.astype(BF16)
    far_copies = []
    for dh in range(1, heads):
        to_head = (head + dh) % heads
        their_rows = pl.ds(pl.multiple_of(to_head * 16, 16), 16)
        far_copies.append(push(s.far_out.at[their_rows], s.far_in.at[head], s.far_sem, dh - 1, rep, to_head))
    s.far_in[head] = s.far_out[pl.ds(pl.multiple_of(head * 16, 16), 16), :]
    cols_pass.wait_recv()
    static_pass.wait_recv()
    row = iota((width, width), 0)
    col = iota((width, width), 1)
    squeeze = one_hot((row < line_columns) & (col == row + (pitch - columns) * ((row * 2341) >> 16)))
    for i in range(head_features // 512):
        cut = pl.ds(512 * i, 512)
        s.cols[:, cut] = nn(squeeze, s.cols_in[:, cut]).astype(BF16)
    static = nn(squeeze, s.static_in[...]).astype(BF16)
    s.residual_c[...] = nt(reorder, static[:, :tokens])
    their_expert = iota((lines, experts), 0) * (CORES * heads) + owner
    pick = one_hot(iota((lines, experts), 1) == their_expert)
    s.centroid_c[...] = nt(pick, static[:, tok_lanes:tok_lanes + experts])
    first = one_hot((iota((8, 128), 0) == 0) & (iota((8, 128), 1) == 0))
    s.gain_c[...] = nt(first, static[:, tok_lanes + exp_lanes:])
    for copy in far_copies:
        copy.wait_recv()
    extras = [s.far_in[h, :, pl.ds(kv, 128)].astype(F32) for h in range(heads)]
    maxima = [extra[:, 0:1] + extra[:, 1:2] + extra[:, 2:3] for extra in extras]
    top = functools.reduce(jnp.maximum, maxima)
    total = jnp.zeros((16, kv), F32)
    weight_sum = jnp.zeros((16, 1), F32)
    for h in range(heads):
        factor = jnp.exp(maxima[h] - top)
        total = total + factor * s.far_in[h, :, pl.ds(0, kv)].astype(F32)
        weight_sum = weight_sum + factor * (extras[h][:, 3:4] + extras[h][:, 4:5])
    keep_latents(RES, total / weight_sum)
    s.far_heads_out[...] = head_outputs(RES, 1)
    far_head_copies = []
    for k, (dx, dz) in enumerate(line_offsets):
        far_head_copies.append(push(s.far_heads_out, s.far_heads_in.at[line], s.heads_sem, k, rep_at(dx, dz, 0), head))
    s.far_heads_in[line] = s.far_heads_out[...]


    def project(copies, arrived, wide, count):
        for copy in copies:
            copy.wait_recv()
        wide[...] = arrived[...].astype(F32).reshape(wide.shape)
        acts = [wide[pl.ds(h, count, stride=16), :].astype(BF16) for h in range(16)]
        return nt(jnp.concatenate(acts, axis=1), s.cols[...])

    def spread_sum(part):
        s.sum_out[...] = part.astype(BF16)
        return [
            push(s.sum_out, s.sum_in.at[dh - 1], s.near_sum_sem, dh - 1, rep, (head + dh) % heads)
            for dh in range(1, heads)
        ]

    def swap_sum(part, copies):
        for dh, copy in enumerate(copies):
            copy.wait_recv()
            part = part + s.sum_in[dh].astype(F32)
        s.swap_out[...] = part
        return push(s.swap_out, s.swap_in, s.swap_sem, 0, other, head)

    near_part = project(near_copies, s.near_in, s.near_w, near)
    near_sums = spread_sum(near_part)
    far_part = project(far_head_copies, s.far_heads_in, s.far_w, lines)
    s.far_sum_out[...] = far_part.astype(BF16)
    far_sums = []
    for k, (dc, dh) in enumerate(line_places):
        far_sums.append(push(s.far_sum_out, s.far_sum_in.at[k], s.sum_sem, k, rep_at(0, 0, dc), (head + dh) % heads))
    near_swap = swap_sum(near_part, near_sums)
    first_core = core == 0
    near_tokens = CORES * near
    near_swap.wait_recv()

    def by_core(mine, theirs):
        return jnp.concatenate([jnp.where(first_core, mine, theirs), jnp.where(first_core, theirs, mine)], axis=0)

    def scaled_rows(attended, start, count):
        here = pl.ds(start, count)
        combined = s.residual_c[here, :] + attended
        s.combined[here, :] = combined
        square_high, square_low = split2(jnp.sum(combined * combined, axis=1, keepdims=True))
        scaled = combined * s.gain_c[0:1, :]
        token_lane = iota((count, width), 1)
        scaled = jnp.where(token_lane == line_columns, square_high, scaled)
        return jnp.where(token_lane == line_columns + 1, square_low, scaled).astype(BF16)

    near_scaled = scaled_rows(by_core(s.swap_out[...], s.swap_in[...]), 0, near_tokens)
    gathered = nn(s.gather_held[:, pl.ds(0, near_tokens)], near_scaled)
    far_mine = far_part
    far_theirs = jnp.zeros_like(far_part)
    for k, (dc, dh) in enumerate(line_places):
        far_sums[k].wait_recv()
        if dc == 0:
            far_mine = far_mine + s.far_sum_in[k].astype(F32)
        else:
            far_theirs = far_theirs + s.far_sum_in[k].astype(F32)
    far_scaled = scaled_rows(by_core(far_mine, far_theirs), near_tokens, CORES * lines)
    gathered = gathered + nn(s.gather_held[:, pl.ds(near_tokens, CORES * lines)], far_scaled)
    slot_lane = iota((SLOTS, width), 1)
    s.gathered[...] = gathered

    def fill_rows(to_line):
        rows = s.gathered[pl.ds(pl.multiple_of(to_line * SLOTS, SLOTS), SLOTS), :]
        high, low = split2(jnp.sum(rows * s.centroid_c[pl.ds(to_line, 1), :], axis=1, keepdims=True))
        rows = jnp.where(slot_lane == line_columns + 2, high, rows)
        rows = jnp.where(slot_lane == line_columns + 3, low, rows)
        return rows.astype(BF16)

    tok_copies = []
    for k, (dx, dz) in enumerate(line_offsets):
        to_line = line_at(dx, dz)
        s.tok_out[to_line] = fill_rows(to_line)
        tok_copies.append(push(s.tok_out.at[to_line], s.tok_in.at[line], s.tok_sem, k, rep_at(dx, dz, 0), head))
    s.tok_in[line] = fill_rows(line)
    sent = rows_copies + cols_copies + static_copies + [cols_pass, static_pass] + query_copies + far_copies
    sent += near_copies + far_head_copies + near_sums + far_sums + [near_swap]
    for copy in sent:
        copy.wait_send()

    load_up.wait()
    inner = nn(s.tok_in[line][:, :line_columns], s.up[line])
    stats = s.tok_in[line].astype(F32)[:, width - 128:]
    for copy, (dx, dz) in zip(tok_copies, line_offsets):
        copy.wait_recv()
        from_line = line_at(-dx, -dz)
        rows = s.tok_in[from_line]
        inner = inner + nn(rows[:, :line_columns], s.up[from_line])
        stats = stats + rows.astype(F32)[:, width - 128:]
    at = line_columns - (width - 128)
    squares = stats[:, at:at + 1] + stats[:, at + 1:at + 2]
    logit = stats[:, at + 2:at + 3] + stats[:, at + 3:at + 4]
    root_mean = jnp.sqrt(squares / features + 1e-6)
    inner = inner / root_mean
    hidden = (inner * jax.nn.sigmoid(inner)).astype(BF16)
    affinity = jax.nn.sigmoid(logit / root_mean)
    affinity_high, affinity_low = split2(affinity)
    for copy in load_down:
        copy.wait()
    back_copies = []

    def steps_to(offset):
        return min(offset[0], xs - offset[0]) + min(offset[1], zs - offset[1])

    def send_back(places):
        for k in places:
            dx, dz = line_offsets[k]
            back_copies.append(push(s.back_out.at[line_at(dx, dz)], s.back_in.at[line], s.back_sem, k, rep_at(dx, dz, 0), head))

    filler = jnp.zeros((SLOTS, width - line_columns), F32)
    x_order = sorted(range(xs), key=lambda dx: -min(dx, xs - dx))
    for dx in x_order:
        to_x = (lx + dx) % xs
        result = nn(hidden, s.down[to_x]) * affinity
        for z in range(zs):
            piece = jnp.concatenate([result[:, z * line_columns:(z + 1) * line_columns], filler], axis=1)
            piece = jnp.where(slot_lane == line_columns, affinity_high, piece)
            piece = jnp.where(slot_lane == line_columns + 1, affinity_low, piece)
            s.back_out[to_x * zs + z] = piece.astype(BF16)
        send_back([k for k, offset in enumerate(line_offsets) if offset[0] == dx and steps_to(offset) > 2])
    send_back([k for k, offset in enumerate(line_offsets) if steps_to(offset) <= 2])
    s.back_in[line] = s.back_out[line]
    rest = s.combined[...]
    my_columns = one_hot((iota((pitch, width), 0) < columns) & (iota((pitch, width), 1) == owner * columns + iota((pitch, width), 0)))
    combined_own = jnp.zeros((pitch, tokens), F32)
    for _ in range(3):
        part = rest.astype(BF16)
        rest = rest - part.astype(F32)
        combined_own = combined_own + nn(nt(my_columns, part).astype(BF16), s.reorder[...])
    s.combined_own[...] = combined_own

    for copy in tok_copies:
        copy.wait_send()
    for copy in back_copies:
        copy.wait_recv()

    returned = jnp.concatenate([s.back_in[e].astype(F32) for e in range(lines)], axis=0).astype(BF16)
    summed = nn(s.scatter[...], returned)
    token_lane = iota((tokens, width), 1)
    share_high, share_low = split2(summed[:, line_columns:line_columns + 1] + summed[:, line_columns + 1:line_columns + 2])
    summed = jnp.where(token_lane == line_columns, share_high, summed)
    summed = jnp.where(token_lane == line_columns + 1, share_low, summed)
    place_in = row & (pitch - 1)
    wanted = jnp.where(place_in < columns, row - (pitch - columns) * (row // pitch), line_columns + place_in - columns)
    spread = one_hot((col == wanted) & (place_in < columns + 2))
    pieces = nt(spread, summed.astype(BF16)).astype(BF16)
    for j in range(CORES * heads):
        s.last_out[j] = pieces[pitch * j:pitch * j + pitch]
    last_copies = []
    for k, (dc, dh) in enumerate(line_places):
        to_core, to_head = (core + dc) % CORES, (head + dh) % heads
        last_copies.append(push(
            s.last_out.at[to_core * heads + to_head], s.last_in.at[owner], s.last_sem, k, rep_at(0, 0, dc), to_head))
    s.last_in[owner] = s.last_out[owner]
    for copy in back_copies:
        copy.wait_send()
    for copy in last_copies:
        copy.wait_recv()
    routed = s.last_in[0].astype(F32)
    for j in range(1, CORES * heads):
        routed = routed + s.last_in[j].astype(F32)
    share = routed[columns:columns + 1] + routed[columns + 1:columns + 2]
    layer_out = s.combined_own[...] + 2.5 * routed / share
    out_ref[...] = layer_out[:columns].astype(BF16)

    for copy in last_copies:
        copy.wait_send()


def per_device(
    query, latent_cache, moved_rows, target_group, moved_length, key_absorb, value_head_projection,
    out_proj, residual, norm_gain, centroid, expert_ids, up_weight, down_weight,
):
    reps = lax.axis_size("rep")
    heads = lax.axis_size("head")
    lines = reps // CORES
    xs = 4 if lines % 4 == 0 else lines
    zs = lines // xs
    groups, moved_n, full = moved_rows.shape
    batch, local_heads, qdim = query.shape
    columns = out_proj.shape[1]
    tokens, topk = expert_ids.shape
    features, hidden = up_weight.shape[1:]
    experts = centroid.shape[0]
    kv = value_head_projection.shape[1]
    vd = value_head_projection.shape[2]
    context = latent_cache.shape[1]
    line_columns = columns * CORES * heads
    width = -(-line_columns // 128) * 128
    pitch = -(-columns // 16) * 16
    half = tokens // CORES
    tok_lanes = -(-tokens // 128) * 128
    static_lanes = tok_lanes + -(-experts // 128) * 128 + 128
    head_features = local_heads * vd

    vmem = dict(
        target=((1, groups), jnp.int32),
        length=((1, groups), jnp.int32),
        source_v=((groups, 128), jnp.int32),
        moved=((groups, moved_n, full), BF16),
        moved_out=((groups, moved_n, full), BF16),
        moved_in=((reps, moved_n, full), BF16),
        rows_b=((reps * moved_n, full), BF16),
        query=((batch * local_heads, qdim), BF16),
        query_f=((batch * local_heads, 128), F32),
        absorb=(key_absorb.shape, BF16),
        value=(value_head_projection.shape, BF16),
        cache=((latent_cache.shape[0], full, context), BF16),
        outproj=((columns, out_proj.shape[0]), BF16),
        cols_out=((pitch, out_proj.shape[0]), BF16),
        cols_in=((pitch * CORES * heads, head_features), BF16),
        cols=((width, head_features), BF16),
        residual=((columns, tokens), BF16),
        gain=((1, columns), BF16),
        centroid=((columns, experts), BF16),
        ids=((topk, tokens), jnp.int32),
        static_out=((pitch, static_lanes), BF16),
        static_in=((pitch * CORES * heads, static_lanes), BF16),
        residual_c=((tokens, width), F32),
        centroid_c=((lines, width), F32),
        gain_c=((8, width), F32),
        reorder=((tokens, tokens), BF16),
        gather=((lines * SLOTS, tokens), BF16),
        gather_held=((lines * SLOTS, tokens), BF16),
        scatter=((tokens, lines * SLOTS), BF16),
        joined=((kv // 128 + 1, batch * local_heads, 128), F32),
        latents=((kv // 128, batch * local_heads, 128), F32),
        heads_f=((batch * local_heads, vd), F32),
        near_out=((RES * local_heads, vd), BF16),
        near_in=((lines, RES * local_heads, vd), BF16),
        near_w=((lines * RES * local_heads, vd), F32),
        far_heads_out=((local_heads, vd), BF16),
        far_heads_in=((lines, local_heads, vd), BF16),
        far_w=((lines * local_heads, vd), F32),
        far_query=((local_heads, full), BF16),
        far_queries=((heads, local_heads, full), BF16),
        far_out=((heads * local_heads, kv + 128), BF16),
        far_in=((heads, local_heads, kv + 128), BF16),
        sum_out=((lines * RES, width), BF16),
        sum_in=((heads - 1, lines * RES, width), BF16),
        far_sum_out=((lines, width), BF16),
        far_sum_in=((CORES * heads - 1, lines, width), BF16),
        swap_out=((lines * RES, width), F32),
        swap_in=((lines * RES, width), F32),
        combined=((tokens, width), F32),
        combined_own=((pitch, tokens), F32),
        gathered=((lines * SLOTS, width), F32),
        tok_out=((lines, SLOTS, width), BF16),
        tok_in=((lines, SLOTS, width), BF16),
        up=((lines, line_columns, hidden), BF16),
        down=((xs, hidden, zs * line_columns), BF16),
        back_out=((lines, SLOTS, width), BF16),
        back_in=((lines, SLOTS, width), BF16),
        last_out=((CORES * heads, pitch, tokens), BF16),
        last_in=((CORES * heads, pitch, tokens), BF16),
    )
    sems = dict(
        load_sem=(16 + xs,), rows_sem=(2, reps - 1), cols_sem=(2, heads), static_sem=(2, heads),
        query_sem=(2, heads - 1), far_sem=(2, heads - 1), heads_sem=(2, lines - 1), sum_sem=(2, CORES * heads - 1),
        swap_sem=(2, 1), near_sem=(2, lines - 1), near_sum_sem=(2, heads - 1), tok_sem=(2, lines - 1), back_sem=(2, lines - 1), last_sem=(2, CORES * heads - 1),
    )
    names = list(vmem) + ["source_s"] + list(sems)
    scratch = [pltpu.VMEM(shape, dtype) for shape, dtype in vmem.values()]
    scratch += [pltpu.SMEM((groups, 128), jnp.int32)]
    scratch += [pltpu.SemaphoreType.DMA(shape) for shape in sems.values()]
    dims = (reps, heads, lines, xs, zs, groups, moved_n, columns, tokens, features)
    layer_out = pl.pallas_call(
        functools.partial(layer_kernel, names, dims),
        out_shape=jax.ShapeDtypeStruct((columns, tokens), BF16),
        in_specs=[pl.BlockSpec(memory_space=pl.ANY)] * 14,
        out_specs=pl.BlockSpec(memory_space=pltpu.VMEM),
        scratch_shapes=scratch,
        compiler_params=pltpu.CompilerParams(
            collective_id=0, has_side_effects=True, vmem_limit_bytes=60 * 1024 * 1024
        ),
        name="latent_moe_layer",
    )(
        target_group.reshape(1, groups), moved_length.reshape(1, groups), query.reshape(batch * local_heads, qdim), jnp.swapaxes(latent_cache, 1, 2), moved_rows,
        key_absorb, value_head_projection, out_proj.T, residual.T, norm_gain.reshape(1, columns), centroid.T,
        expert_ids.T, up_weight.reshape(lines, line_columns, hidden), down_weight[0],
    )
    return layer_out.T


def solution(mesh):
    return jax.shard_map(
        per_device,
        mesh=mesh,
        in_specs=(
            P("rep", "head", None),
            P("rep", None, None),
            P(None, ("rep", "head"), None),
            P(),
            P(),
            P("head", None, None),
            P("head", None, None),
            P(None, ("rep", "head")),
            P(None, ("rep", "head")),
            P(("rep", "head")),
            P(None, ("rep", "head")),
            P(),
            P(("rep", "head"), None, None),
            P(("rep", "head"), None, None),
        ),
        out_specs=P(None, ("rep", "head")),
        check_vma=False,
    )
```
